128 devices in a mesh: ctx: 16 (over y, z_lo, core), kv: 8 (over x, z_hi).
Axes of the slice: x: 4, y: 4, z: 4 (z_hi: 2, z_lo: 2; z = z_hi * 2 + z_lo), core: 2. Of those that a mesh axis runs over, the one named last changes fastest.
Arguments:
- prompt_in: bfloat16 [256, 8192], P(None, 'ctx'), may hold values from -6 to 6
- step_in: bfloat16 [3, 64, 8192], P(None, None, 'ctx'), may hold values from -6 to 6
- norm_gain: bfloat16 [8192], P('ctx'), may hold values from 0.099609375 to 1.8984375
- query_weight: bfloat16 [8192, 8192], P('ctx', 'kv'), may hold values from -0.125 to 0.125
- key_weight: bfloat16 [8192, 1024], P('ctx', 'kv'), may hold values from -0.125 to 0.125
- value_weight: bfloat16 [8192, 1024], P('ctx', 'kv'), may hold values from -0.0625 to 0.0625
- out_weight: bfloat16 [8192, 8192], P('kv', 'ctx'), may hold values from -0.125 to 0.125
- key_cache: bfloat16 [8, 131072, 128], P('kv', 'ctx'), may hold values from -540 to 540
- value_cache: bfloat16 [8, 131072, 128], P('kv', 'ctx'), may hold values from -5 to 5
- cache_lengths: int32 [16], P('ctx'), may hold values from 2048 to 8192
- visible: int32 [64], replicated, may hold values from 1 to 256, as said below
Outputs:
- prompt_out: bfloat16 [256, 8192], P('kv', 'ctx')
- step_out: bfloat16 [3, 64, 8192], P(None, 'kv', 'ctx')
The draws below stay inside these ranges and needn't reach their ends.
Inputs may be any that keep to these rules, and one draw needn't show every extreme that they name: `visible`: prompt tokens seen by each decode row.
All inputs are finite; a program needn't handle non-finite values.
Results may differ from the reference program's by a relative error of at most 0.035.
Values may be sent and summed in bfloat16 or wider, within the bound.
A program may use at most 192 MiB of HBM per device.

```python
import jax
import jax.numpy as jnp
from jax import lax

D = 8192
HD = 128
QPK = 8
KV_HEADS = 8
CACHE_DEV = 8192
PROMPT_DEV = 16
ROWS_DEV = 4
STEPS = 3
SHARDS = 16
CACHE = 131072
PROMPT = 256
ROWS = 64


def draw_key_cache(key, part):
    entries = jnp.clip(jax.random.normal(key, (KV_HEADS, CACHE, HD), jnp.float32), -6.0, 6.0) * 1.5
    return entries.astype(jnp.bfloat16)


def draw_value_cache(key, part):
    jitter = jnp.clip(jax.random.normal(key, (KV_HEADS, SHARDS, CACHE_DEV, HD), jnp.float32), -4.0, 4.0)
    centers = jax.random.uniform(jax.random.fold_in(key, 21), (KV_HEADS, SHARDS, 1, HD), jnp.float32, -1.0, 1.0)
    return (jitter + centers).reshape(KV_HEADS, CACHE, HD).astype(jnp.bfloat16)


def draw_cache_lengths(key, part):
    lengths = jax.random.randint(key, (SHARDS,), CACHE_DEV // 4, CACHE_DEV + 1)
    full_shard = jax.random.randint(jax.random.fold_in(key, 31), (), 0, SHARDS)
    short_shard = (full_shard + 1 + jax.random.randint(jax.random.fold_in(key, 32), (), 0, SHARDS - 1)) % SHARDS
    shard_ids = jnp.arange(SHARDS, dtype=jnp.int32)
    lengths = jnp.where(shard_ids == full_shard, CACHE_DEV, lengths)
    lengths = jnp.where(shard_ids == short_shard, CACHE_DEV // 4, lengths)
    return lengths.astype(jnp.int32)


def draw_visible(key, part):
    counts = jax.random.randint(key, (ROWS,), 1, PROMPT + 1)
    ranking = jax.random.permutation(jax.random.fold_in(key, 41), ROWS)
    counts = jnp.where(ranking == 0, PROMPT, counts)
    counts = jnp.where(ranking == 1, 1, counts)
    return counts.astype(jnp.int32)


def shard_levels(key, shape, shards, least, high):
    def one(dim, parts):
        draws = jax.random.uniform(jax.random.fold_in(jax.random.fold_in(key, 6), dim), (parts,), jnp.float32, least / len(shards), high / len(shards))
        return jnp.repeat(jnp.exp(draws), shape[dim] // parts).reshape((-1,) + (1,) * (len(shape) - dim - 1))

    gain = one(*shards[0])
    for cut in shards[1:]:
        gain = gain * one(*cut)
    return gain


def normal_values(stream_key, extent, deviation, bound, shards=(), held_as=jnp.bfloat16):
    values = jax.random.normal(stream_key, extent, jnp.float32) * deviation
    if len(shards) > 0:
        values = shard_levels(stream_key, extent, shards, -0.22, 0.18) * values
    return jnp.clip(values, min=-bound, max=bound).astype(held_as)


def setup_inputs(seed: int = 0) -> dict:
    seeds = jax.random.split(jax.random.key(seed), 12)
    prompt_in = normal_values(seeds[0], (PROMPT, D), 1.0, 6.0, ((1, 16),))
    step_in = normal_values(seeds[1], (STEPS, ROWS, D), 1.0, 6.0, ((2, 16),))
    norm_gain = jnp.clip(1.0 + 0.18 * jax.random.normal(seeds[2], (D,), jnp.float32), 0.099609375, 1.8984375).astype(jnp.bfloat16)
    query_weight = normal_values(seeds[3], (D, KV_HEADS * QPK * HD), (D // 4) ** -0.5, 0.125, ((0, 16), (1, 8)))
    key_weight = normal_values(seeds[4], (D, KV_HEADS * HD), (D // 4) ** -0.5, 0.125, ((0, 16), (1, 8)))
    value_weight = normal_values(seeds[5], (D, KV_HEADS * HD), D ** -0.5, 0.0625, ((0, 16), (1, 8)))
    out_weight = normal_values(seeds[6], (KV_HEADS * QPK * HD, D), (2 * QPK * HD) ** -0.5, 0.125, ((0, 8), (1, 16)))
    key_cache = draw_key_cache(jax.random.fold_in(seeds[11], 71), 0)
    value_cache = draw_value_cache(jax.random.fold_in(seeds[11], 71), 0)
    cache_lengths = draw_cache_lengths(jax.random.fold_in(seeds[11], 71), 0)
    visible = draw_visible(jax.random.fold_in(seeds[11], 71), 0)
    return dict(prompt_in=prompt_in, step_in=step_in, norm_gain=norm_gain, query_weight=query_weight, key_weight=key_weight, value_weight=value_weight, out_weight=out_weight, key_cache=key_cache, value_cache=value_cache, cache_lengths=cache_lengths, visible=visible)


EPSILON = 1e-05

def project(inputs, norm_gain, weight):
    widened = inputs.astype(jnp.float32)
    scaled = (widened * norm_gain.astype(jnp.float32)).astype(jnp.bfloat16)
    inverse = lax.rsqrt(lax.optimization_barrier(jnp.sum(widened * widened, axis=1)) / D + EPSILON)
    product = jnp.dot(scaled, weight, preferred_element_type=jnp.float32)
    return (product * inverse[:, None]).astype(jnp.bfloat16)

def block_partial(queries, key_shard, value_shard, length, extra_keys, extra_values, extra_mask):
    factor = HD ** (-0.5)
    slots_live = jnp.arange(CACHE_DEV, dtype=jnp.int32)[None, :] < length
    cache_scores = jnp.dot(queries, key_shard.T, preferred_element_type=jnp.float32) * factor
    extra_scores = jnp.dot(queries, extra_keys.T, preferred_element_type=jnp.float32) * factor
    cache_scores = jnp.where(slots_live, cache_scores, -jnp.inf)
    extra_scores = jnp.where(extra_mask, extra_scores, -jnp.inf)
    highest = jnp.maximum(lax.optimization_barrier(jnp.max(cache_scores, axis=1)), lax.optimization_barrier(jnp.max(extra_scores, axis=1)))
    cache_weights = jnp.exp(cache_scores - highest[:, None]).astype(jnp.bfloat16)
    extra_weights = jnp.exp(extra_scores - highest[:, None]).astype(jnp.bfloat16)
    totals = lax.optimization_barrier(jnp.sum(cache_weights.astype(jnp.float32), axis=1)) + lax.optimization_barrier(jnp.sum(extra_weights.astype(jnp.float32), axis=1))
    mixture = jnp.dot(cache_weights, value_shard, preferred_element_type=jnp.float32)
    mixture = mixture + jnp.dot(extra_weights, extra_values, preferred_element_type=jnp.float32)
    return (highest, totals, mixture)

def reference(prompt_in, step_in, norm_gain, query_weight, key_weight, value_weight, out_weight, key_cache, value_cache, cache_lengths, visible):
    row_count = PROMPT + STEPS * ROWS
    every_in = jnp.concatenate([prompt_in, step_in.reshape(STEPS * ROWS, D)], axis=0)
    queries = project(every_in, norm_gain, query_weight).reshape(row_count, KV_HEADS, QPK * HD)
    keys = project(every_in, norm_gain, key_weight).reshape(row_count, KV_HEADS, HD)
    values = project(every_in, norm_gain, value_weight).reshape(row_count, KV_HEADS, HD)
    position = jnp.arange(row_count, dtype=jnp.int32)
    is_prompt = position < PROMPT
    after_prompt = jnp.maximum(position - PROMPT, 0)
    row_index = after_prompt % ROWS
    limits = jnp.where(is_prompt, position + 1, visible[row_index])
    owner_rows = jnp.where(is_prompt, -1, row_index)
    owner_steps = jnp.where(is_prompt, -1, after_prompt // ROWS)
    slot_ids = jnp.arange(PROMPT_DEV + ROWS_DEV * STEPS, dtype=jnp.int32)
    slot_prompt = slot_ids < PROMPT_DEV
    decode_slot = jnp.maximum(slot_ids - PROMPT_DEV, 0)

    def per_head(operands):
        head_queries, head_keys, head_values, cache_keys, cache_values = operands
        flat_queries = head_queries.reshape(row_count * QPK, HD)
        prompt_keys = head_keys[:PROMPT]
        prompt_values = head_values[:PROMPT]
        step_keys = head_keys[PROMPT:].reshape(STEPS, ROWS, HD)
        step_values = head_values[PROMPT:].reshape(STEPS, ROWS, HD)

        def per_block(shard_index):
            key_shard = lax.dynamic_slice_in_dim(cache_keys, shard_index * CACHE_DEV, CACHE_DEV, 0)
            value_shard = lax.dynamic_slice_in_dim(cache_values, shard_index * CACHE_DEV, CACHE_DEV, 0)
            block_keys = lax.dynamic_slice_in_dim(prompt_keys, shard_index * PROMPT_DEV, PROMPT_DEV, 0)
            block_values = lax.dynamic_slice_in_dim(prompt_values, shard_index * PROMPT_DEV, PROMPT_DEV, 0)
            own_keys = jnp.swapaxes(lax.dynamic_slice_in_dim(step_keys, shard_index * ROWS_DEV, ROWS_DEV, 1), 0, 1)
            own_values = jnp.swapaxes(lax.dynamic_slice_in_dim(step_values, shard_index * ROWS_DEV, ROWS_DEV, 1), 0, 1)
            extra_keys = jnp.concatenate([block_keys, own_keys.reshape(ROWS_DEV * STEPS, HD)], axis=0)
            extra_values = jnp.concatenate([block_values, own_values.reshape(ROWS_DEV * STEPS, HD)], axis=0)
            seen_prompt = (shard_index * PROMPT_DEV + slot_ids)[None, :] < limits[:, None]
            seen_own = ((shard_index * ROWS_DEV + decode_slot // STEPS)[None, :] == owner_rows[:, None]) & ((decode_slot % STEPS)[None, :] <= owner_steps[:, None])
            seen_keys = jnp.where(slot_prompt[None, :], seen_prompt, seen_own)
            flat_seen = jnp.repeat(seen_keys, QPK, axis=0)
            return block_partial(flat_queries, key_shard, value_shard, cache_lengths[shard_index], extra_keys, extra_values, flat_seen)
        highest, totals, mixture = lax.map(per_block, jnp.arange(SHARDS, dtype=jnp.int32))
        overall = lax.optimization_barrier(jnp.max(highest, axis=0))
        rescale = jnp.exp(highest - overall[None, :])
        summed = lax.optimization_barrier(jnp.sum(mixture * rescale[:, :, None], axis=0))
        denominator = lax.optimization_barrier(jnp.sum(totals * rescale, axis=0))
        result = (summed / denominator[:, None]).astype(jnp.bfloat16)
        return result.reshape(row_count, QPK * HD)
    attended = lax.map(per_head, (jnp.swapaxes(queries, 0, 1), jnp.swapaxes(keys, 0, 1), jnp.swapaxes(values, 0, 1), key_cache, value_cache))
    attended = jnp.swapaxes(attended, 0, 1).reshape(row_count, KV_HEADS * QPK * HD)
    output = jnp.dot(attended, out_weight, preferred_element_type=jnp.float32).astype(jnp.bfloat16)
    return (output[:PROMPT], output[PROMPT:].reshape(STEPS, ROWS, D))
```

```python
import jax
import jax.numpy as jnp
from jax import lax
from jax.experimental import pallas as pl
from jax.experimental.pallas import tpu as pltpu
from jax.sharding import PartitionSpec as P

D = 8192
HD = 128
EPSILON = 1e-05
MESH = pl.DeviceIdType.MESH
F32 = jnp.float32
BF16 = jnp.bfloat16

CTX = 16
KV = 8
CHIPS = 8
GROUP = 56
PROMPT_G = 32
ROWS_G = 8
STEPS = 3
ALL = CHIPS * GROUP
FEAT = 512
PARTS = 2
WIDE = 512 // PARTS
HEADS_P = WIDE // HD
FLAT = HEADS_P * GROUP
BLOCK = 4 * FLAT
SLOTS = 8192
TILE = 512
TILES = SLOTS // TILE
LOG2E = 1.4426950408889634
HIDDEN = -1e30


def kernel(
    prompt_ref,
    step_ref,
    gain_ref,
    wq_hbm,
    wk_hbm,
    wv_hbm,
    wo_hbm,
    key_hbm,
    value_hbm,
    length_ref,
    visible_ref,
    prompt_out,
    step_out,
    x_raw,
    gain,
    xs,
    wq,
    wkv,
    wo,
    k_raw,
    k_t,
    v_x,
    kx_t,
    vx_x,
    bias,
    inv,
    po,
    kvp,
    a0_send,
    a0_recv,
    kv0_send,
    kv0_recv,
    sq0_send,
    sq0_recv,
    a1_send,
    a1_recv,
    kv1_send,
    kv1_recv,
    sq1_send,
    sq1_recv,
    q_all,
    s_buf,
    sx_buf,
    mx,
    own_mix,
    own_row,
    b0_send,
    b0_recv,
    b1_send,
    b1_recv,
    att,
    o_acc,
    c_send,
    c_recv,
    load_sem,
    p_send,
    p_recv,
    a1_ss,
    a1_rs,
    kv1_ss,
    kv1_rs,
    sq1_ss,
    sq1_rs,
    qg_ss,
    qg_rs,
    qf_ss,
    qf_rs,
    b1_ss,
    b1_rs,
    ag_ss,
    ag_rs,
    af_ss,
    af_rs,
    c_ss,
    c_rs,
):
    c = lax.axis_index("ctx")
    k = lax.axis_index("kv")
    core = lax.rem(c, 2)
    j = lax.div(c, 2)
    other = 1 - core
    sib = (c + 1 - 2 * core, k)

    def chip(jt):
        return (2 * jt + core, k)

    def away(d):
        return lax.rem(j + d, CHIPS)

    def remote(src, dst, ss, rs, dev):
        return pltpu.make_async_remote_copy(
            src_ref=src, dst_ref=dst, send_sem=ss, recv_sem=rs, device_id=dev, device_id_type=MESH
        )

    loads = [pltpu.make_async_copy(prompt_ref, x_raw.at[:, 0:PROMPT_G], load_sem.at[0])]
    for s in range(STEPS):
        low = PROMPT_G + s * ROWS_G
        loads.append(
            pltpu.make_async_copy(step_ref.at[s], x_raw.at[:, low : low + ROWS_G], load_sem.at[1 + s])
        )
    loads.append(pltpu.make_async_copy(gain_ref, gain, load_sem.at[4]))
    loads.append(pltpu.make_async_copy(wq_hbm, wq, load_sem.at[5]))
    loads.append(pltpu.make_async_copy(wk_hbm, wkv.at[:, 0:HD], load_sem.at[6]))
    loads.append(pltpu.make_async_copy(wv_hbm, wkv.at[:, HD : 2 * HD], load_sem.at[7]))
    key_load = pltpu.make_async_copy(key_hbm, k_raw, load_sem.at[8])
    value_load = pltpu.make_async_copy(value_hbm, v_x.at[:, 0:HD], load_sem.at[9])
    wo_load = pltpu.make_async_copy(wo_hbm, wo, load_sem.at[10])
    for copy in loads:
        copy.start()
    key_load.start()
    value_load.start()
    wo_load.start()

    barrier = pltpu.get_barrier_semaphore()
    pl.semaphore_signal(barrier, inc=1, device_id=sib, device_id_type=MESH)
    for d in range(1, CHIPS):
        pl.semaphore_signal(barrier, inc=1, device_id=chip(away(d)), device_id_type=MESH)
        pl.semaphore_signal(
            barrier, inc=1, device_id=(c, lax.rem(k + d, KV)), device_id_type=MESH
        )

    eye_flat = lax.broadcasted_iota(jnp.int32, (FLAT, HD), 0) == lax.broadcasted_iota(
        jnp.int32, (FLAT, HD), 1
    )
    eye_group = lax.broadcasted_iota(jnp.int32, (GROUP, HD), 0) == lax.broadcasted_iota(
        jnp.int32, (GROUP, HD), 1
    )

    def as_row(eye, column):
        return jnp.sum(jnp.where(eye, column, 0.0), axis=0, keepdims=True)

    def as_column(eye, row):
        return jnp.sum(jnp.where(eye, row, 0.0), axis=1, keepdims=True)

    for copy in loads:
        copy.wait()
    xf = x_raw[...].astype(F32).reshape(ALL, FEAT)
    xs[...] = (xf * gain[...].astype(F32)).astype(BF16)
    squares = jnp.sum(xf * xf, axis=1, keepdims=True)
    for g in range(CHIPS):
        sq0_send[g] = as_row(eye_group, squares[g * GROUP : (g + 1) * GROUP])
    pl.semaphore_wait(barrier, 2 * CHIPS - 1)

    def first(p):
        return remote(a0_send.at[p], a0_recv.at[p], p_send.at[p], p_recv.at[p], sib)

    def project(column):
        return jnp.dot(
            xs[...], wq[:, pl.ds(pl.multiple_of(column, HD), WIDE)], preferred_element_type=F32
        )

    kv_first = remote(kv0_send, kv0_recv, p_send.at[PARTS], p_recv.at[PARTS], sib)
    sq_first = remote(sq0_send, sq0_recv, p_send.at[PARTS + 1], p_recv.at[PARTS + 1], sib)
    sq_first.start()
    for p in range(PARTS):
        a0_send[p] = project(other * 512 + p * WIDE).astype(BF16)
        first(p).start()
        if p == 0:
            pairs = jnp.dot(xs[...], wkv[...], preferred_element_type=F32)
            pairs = pairs.reshape(CHIPS, GROUP, 2 * HD)
            of_prompt = pairs[:, 0:PROMPT_G]
            of_steps = jnp.concatenate(
                [pairs[:, PROMPT_G:], jnp.zeros((CHIPS, 8, 2 * HD), F32)], axis=1
            )
            kv0_send[...] = jnp.where(core == 0, of_steps, of_prompt).astype(BF16)
            kv_first.start()
            kvp[...] = jnp.where(core == 0, of_prompt, of_steps)
        po[p] = project(core * 512 + p * WIDE)

    length = length_ref[0]

    def prepare_keys(t, carry):
        low = pl.multiple_of(t * TILE, TILE)
        live = (lax.broadcasted_iota(jnp.int32, (TILE, HD), 0) + low) < length
        keys = jnp.where(live, k_raw[pl.ds(low, TILE)].astype(F32), k_raw[0:1].astype(F32))
        k_t[:, pl.ds(low, TILE)] = keys.astype(BF16).T
        return carry

    def prepare_values(t, carry):
        low = pl.multiple_of(t * TILE, TILE)
        live = (lax.broadcasted_iota(jnp.int32, (TILE, HD), 0) + low) < length
        v_x[pl.ds(low, TILE), 0:HD] = jnp.where(
            live, v_x[pl.ds(low, TILE), 0:HD].astype(F32), 0.0
        ).astype(BF16)
        v_x[pl.ds(low, TILE), HD : 2 * HD] = jnp.where(live, 1.0, 0.0).astype(BF16)
        return carry

    def a1_copy(p, jt, slot):
        return remote(
            a1_send.at[p, jt], a1_recv.at[p, slot], a1_ss.at[p, jt], a1_rs.at[p, slot], chip(jt)
        )

    def kv1_copy(jt, slot):
        return remote(kv1_send.at[jt], kv1_recv.at[slot], kv1_ss.at[jt], kv1_rs.at[slot], chip(jt))

    def sq1_copy(jt, slot):
        return remote(sq1_send.at[jt], sq1_recv.at[slot], sq1_ss.at[jt], sq1_rs.at[slot], chip(jt))

    def spread(p):
        first(p).wait_recv()
        total = po[p] + a0_recv[p].astype(F32)
        a1_send[p] = total.reshape(CHIPS, GROUP, WIDE).astype(BF16)
        for d in range(1, CHIPS):
            a1_copy(p, away(d), j).start()

    def spread_small():
        sq_first.wait_recv()
        sq1_send[...] = sq0_send[...] + sq0_recv[...]
        kv_first.wait_recv()
        kv1_send[...] = (kvp[...] + kv0_recv[...].astype(F32)).astype(BF16)
        for d in range(1, CHIPS):
            sq1_copy(away(d), j).start()
            kv1_copy(away(d), j).start()

    def small_sums():
        square = sq1_send[j]
        for d in range(1, CHIPS):
            src = away(d)
            sq1_copy(src, src).wait_recv()
            square = square + sq1_recv[src]
        inverse = lax.rsqrt(square / D + EPSILON)
        inv[...] = jnp.broadcast_to(as_column(eye_group, inverse), (GROUP, HD))

    def pair_sums():
        pair = kv1_send[j].astype(F32)
        for d in range(1, CHIPS):
            src = away(d)
            kv1_copy(src, src).wait_recv()
            pair = pair + kv1_recv[src].astype(F32)
        inv_steps = jnp.concatenate([inv[PROMPT_G:], jnp.zeros((8, HD), F32)], axis=0)
        scale = jnp.where(core == 0, inv[0:PROMPT_G], inv_steps)
        blank = jnp.zeros((HD - PROMPT_G, HD), F32)
        new_keys = jnp.concatenate([pair[:, 0:HD] * scale, blank], axis=0)
        new_values = jnp.concatenate([pair[:, HD:] * scale, blank], axis=0)
        kx_t[...] = new_keys.T.astype(BF16)
        vx_x[:, 0:HD] = new_values.astype(BF16)
        vx_x[:, HD : 2 * HD] = jnp.ones((HD, HD), BF16)

    def q_copy(p, jt, slot):
        return remote(
            q_all.at[p, core, slot],
            q_all.at[p, core, slot],
            qg_ss.at[p, jt],
            qg_rs.at[p, slot],
            chip(jt),
        )

    def q_forward(p, column, slot):
        return remote(
            q_all.at[p, column, slot],
            q_all.at[p, column, slot],
            qf_ss.at[p, slot],
            qf_rs.at[p, slot],
            sib,
        )

    def query_sums(p):
        total = a1_send[p, j].astype(F32)
        for d in range(1, CHIPS):
            src = away(d)
            a1_copy(p, src, src).wait_recv()
            total = total + a1_recv[p, src].astype(F32)
        scale = inv[...] * (HD**-0.5 * LOG2E)
        flat = jnp.concatenate(
            [total[:, h * HD : (h + 1) * HD] * scale for h in range(HEADS_P)], axis=0
        )
        q_all[p, core, j] = flat.astype(BF16)
        for d in range(1, CHIPS):
            q_copy(p, away(d), j).start()
        q_forward(p, core, j).start()

    def forward_queries(p):
        for d in range(1, CHIPS):
            src = away(d)
            q_copy(p, src, src).wait_recv()
            q_forward(p, core, src).start()

    def await_queries(p):
        for slot in range(CHIPS):
            q_forward(p, other, slot).wait_recv()

    def prepare_bias():
        lane = lax.broadcasted_iota(jnp.int32, (GROUP, HD), 1)
        sub = lax.broadcasted_iota(jnp.int32, (GROUP, HD), 0)
        sub8 = lax.broadcasted_iota(jnp.int32, (ROWS_G, HD), 0)
        position = j * PROMPT_G + lane
        key_row = j * ROWS_G + lax.rem(lane, ROWS_G)
        key_step = lax.div(lane, ROWS_G)
        past = sub - PROMPT_G
        is_step = past >= 0
        query_step = lax.div(jnp.maximum(past, 0), ROWS_G)
        for g in range(CHIPS):
            seen_by_row = jnp.zeros((ROWS_G, HD), jnp.int32)
            for b in range(ROWS_G):
                seen_by_row = jnp.where(sub8 == b, visible_ref[g * ROWS_G + b], seen_by_row)
            by_row = jnp.concatenate(
                [jnp.zeros((PROMPT_G, HD), jnp.int32)] + [seen_by_row] * STEPS, axis=0
            )
            limit = jnp.where(is_step, by_row, g * PROMPT_G + sub + 1)
            query_row = g * ROWS_G + lax.rem(jnp.maximum(past, 0), ROWS_G)
            score_prompt = jnp.where((lane < PROMPT_G) & (position < limit), 0.0, HIDDEN)
            score_steps = jnp.where(
                (lane < STEPS * ROWS_G)
                & is_step
                & (key_row == query_row)
                & (key_step <= query_step),
                0.0,
                HIDDEN,
            )
            both = jnp.where(core == 0, score_prompt, score_steps)
            bias[g] = jnp.concatenate([both] * HEADS_P, axis=0)

    key_load.wait()
    lax.fori_loop(0, TILES // 2, prepare_keys, 0)
    spread(0)
    spread_small()
    prepare_bias()
    lax.fori_loop(TILES // 2, TILES, prepare_keys, 0)
    spread(1)
    small_sums()
    query_sums(0)
    pair_sums()
    value_load.wait()
    lax.fori_loop(0, TILES, prepare_values, 0)
    forward_queries(0)

    def place(n):
        p = lax.div(n, 4)
        part = lax.rem(n, 4)
        mine = lax.rem(p + lax.div(part, 2), 2) == 0
        return p, jnp.where(mine, core, other), lax.rem(part, 2), mine

    def lane_max(scores):
        high = scores[:, 0:HD]
        for u in range(1, scores.shape[1] // HD):
            high = jnp.maximum(high, scores[:, u * HD : (u + 1) * HD])
        return high

    def sweep(n_scores, top):
        if n_scores is not None:
            p, column, half, _ = place(n_scores)
            queries = q_all[p, column, pl.ds(half * 4, 4)].reshape(BLOCK, HD)
            mask = bias[pl.ds(half * 4, 4)].reshape(BLOCK, HD)
        high = None
        mixed = None
        for t in range(TILES + 1):
            cols = slice(t * TILE, (t + 1) * TILE)
            if top is not None:
                old = s_buf[t] if t < TILES else sx_buf[...]
                weights = jnp.exp2(old - top).astype(BF16)
            if n_scores is not None:
                if t < TILES:
                    scores = jnp.dot(queries, k_t[:, cols], preferred_element_type=F32)
                    s_buf[t] = scores
                else:
                    scores = jnp.dot(queries, kx_t[...], preferred_element_type=F32) + mask
                    sx_buf[...] = scores
                peak = lane_max(scores)
                high = peak if high is None else jnp.maximum(high, peak)
            if top is not None:
                values = v_x[cols] if t < TILES else vx_x[...]
                part = jnp.dot(weights, values, preferred_element_type=F32)
                mixed = part if mixed is None else mixed + part
        if n_scores is not None:
            mx[...] = high
        return mixed

    def split3(row):
        one = row.astype(BF16).astype(F32)
        two = (row - one).astype(BF16).astype(F32)
        return one, two, row - one - two

    def packed(mixture, top_row, total_row):
        sub = lax.broadcasted_iota(jnp.int32, (16, HD), 0)
        stats = jnp.zeros((16, HD), F32)
        for i, piece in enumerate(split3(top_row) + split3(total_row)):
            stats = jnp.where(sub == i, piece, stats)
        return jnp.concatenate([mixture, stats], axis=0).astype(BF16)

    def unpacked(packet):
        wide = packet.astype(F32)
        stats = wide[FLAT:]
        return (
            wide[0:FLAT],
            stats[0:1] + stats[1:2] + stats[2:3],
            stats[3:4] + stats[4:5] + stats[5:6],
        )

    def keep(n, mixed, top):
        p, _, half, mine = place(n)
        for i in range(4):
            rows = slice(i * FLAT, (i + 1) * FLAT)
            top_row = as_row(eye_flat, top[rows])
            total_row = as_row(eye_flat, mixed[rows, HD:])

            @pl.when(mine)
            def _():
                own_mix[p, half * 4 + i] = mixed[rows, 0:HD]
                own_row[p, half * 4 + i, 0:1] = top_row
                own_row[p, half * 4 + i, 1:2] = total_row

            @pl.when(jnp.logical_not(mine))
            def _():
                b0_send[p, half * 4 + i] = packed(mixed[rows, 0:HD], top_row, total_row)

    def b0_copy(p):
        return remote(
            b0_send.at[p], b0_recv.at[p], p_send.at[PARTS + 2 + p], p_recv.at[PARTS + 2 + p], sib
        )

    def b1_copy(p, jt, slot):
        return remote(
            b1_send.at[p, jt], b1_recv.at[p, slot], b1_ss.at[p, jt], b1_rs.at[p, slot], chip(jt)
        )

    def merge_pair(p, half):
        for i in range(4):
            jt = half * 4 + i
            mix1, top1, tot1 = unpacked(b0_recv[p, jt])
            top0 = own_row[p, jt, 0:1]
            tot0 = own_row[p, jt, 1:2]
            top = jnp.maximum(top0, top1)
            w0 = jnp.exp2(top0 - top)
            w1 = jnp.exp2(top1 - top)
            mixture = own_mix[p, jt] * as_column(eye_flat, w0) + mix1 * as_column(eye_flat, w1)
            b1_send[p, jt] = packed(mixture, top, w0 * tot0 + w1 * tot1)

            @pl.when(jt != j)
            def _():
                b1_copy(p, jt, j).start()

    def att_copy(p, jt, slot):
        return remote(
            att.at[p, core, slot], att.at[p, core, slot], ag_ss.at[p, jt], ag_rs.at[p, slot], chip(jt)
        )

    def att_forward(p, column, slot):
        return remote(
            att.at[p, column, slot], att.at[p, column, slot], af_ss.at[p, slot], af_rs.at[p, slot], sib
        )

    def merge_all(p):
        pieces = [unpacked(b1_send[p, j])]
        for d in range(1, CHIPS):
            src = away(d)
            b1_copy(p, src, src).wait_recv()
            pieces.append(unpacked(b1_recv[p, src]))
        top = pieces[0][1]
        for piece in pieces[1:]:
            top = jnp.maximum(top, piece[1])
        shares = [jnp.exp2(piece[1] - top) for piece in pieces]
        total = shares[0] * pieces[0][2]
        for share, piece in zip(shares[1:], pieces[1:]):
            total = total + share * piece[2]
        result = jnp.zeros((FLAT, HD), F32)
        for share, piece in zip(shares, pieces):
            result = result + piece[0] * as_column(eye_flat, share)
        result = result * as_column(eye_flat, 1.0 / total)
        att[p, core, j] = jnp.concatenate(
            [result[h * GROUP : (h + 1) * GROUP] for h in range(HEADS_P)], axis=1
        ).astype(BF16)
        for d in range(1, CHIPS):
            att_copy(p, away(d), j).start()
        att_forward(p, core, j).start()

    def forward_attended(p):
        for d in range(1, CHIPS):
            src = away(d)
            att_copy(p, src, src).wait_recv()
            att_forward(p, core, src).start()

    def await_attended(p):
        for slot in range(CHIPS):
            att_forward(p, other, slot).wait_recv()

    def out_part(p, column):
        rows = att[p, column].astype(F32).reshape(ALL, WIDE).astype(BF16)
        low = pl.multiple_of(column * 512 + p * WIDE, WIDE)
        return jnp.dot(rows, wo[pl.ds(low, WIDE)], preferred_element_type=F32)

    def step_top():
        return jnp.max(mx[...], axis=1, keepdims=True)

    sweep(0, None)

    def step(n, carry):
        @pl.when(n == 1)
        def _():
            await_queries(0)
            query_sums(1)

        @pl.when(n == 2)
        def _():
            forward_queries(1)

        @pl.when(n == 3)
        def _():
            await_queries(1)

        @pl.when(n == 4)
        def _():
            b0_copy(0).start()

        @pl.when(n == 5)
        def _():
            b0_copy(0).wait_recv()
            merge_pair(0, 0)
            merge_pair(0, 1)

        @pl.when(n == 6)
        def _():
            b0_copy(1).start()
            merge_all(0)

        top = step_top()
        mixed = sweep(n + 1, top)
        keep(n, mixed, jnp.broadcast_to(top, (BLOCK, HD)))
        return carry

    lax.fori_loop(0, 7, step, 0)
    forward_attended(0)
    b0_copy(1).wait_recv()
    merge_pair(1, 0)
    top = step_top()
    mixed = sweep(None, top)
    keep(7, mixed, jnp.broadcast_to(top, (BLOCK, HD)))
    merge_pair(1, 1)
    await_attended(0)
    wo_load.wait()
    o_acc[...] = out_part(0, 0) + out_part(0, 1)
    merge_all(1)
    forward_attended(1)
    o_acc[...] += out_part(1, core)
    await_attended(1)
    result = o_acc[...] + out_part(1, other)

    def c_copy(kt, slot):
        return remote(c_send.at[kt], c_recv.at[slot], c_ss.at[kt], c_rs.at[slot], (c, kt))

    c_send[...] = result.reshape(KV, GROUP, FEAT).astype(BF16)
    for d in range(1, KV):
        c_copy(lax.rem(k + d, KV), k).start()
    final = c_send[k].astype(F32)
    for d in range(1, KV):
        src = lax.rem(k + d, KV)
        c_copy(src, src).wait_recv()
        final = final + c_recv[src].astype(F32)
    prompt_out[...] = final[0:PROMPT_G].astype(BF16)
    for s in range(STEPS):
        low = PROMPT_G + s * ROWS_G
        step_out[s] = final[low : low + ROWS_G].astype(BF16)

    kv_first.wait_send()
    sq_first.wait_send()
    for p in range(PARTS):
        first(p).wait_send()
        b0_copy(p).wait_send()
        for slot in range(CHIPS):
            q_forward(p, core, slot).wait_send()
            att_forward(p, core, slot).wait_send()
    for d in range(1, CHIPS):
        jt = away(d)
        sq1_copy(jt, j).wait_send()
        kv1_copy(jt, j).wait_send()
        c_copy(lax.rem(k + d, KV), k).wait_send()
        for p in range(PARTS):
            a1_copy(p, jt, j).wait_send()
            q_copy(p, jt, j).wait_send()
            b1_copy(p, jt, j).wait_send()
            att_copy(p, jt, j).wait_send()


def on_device(
    prompt_in,
    step_in,
    norm_gain,
    query_weight,
    key_weight,
    value_weight,
    out_weight,
    key_cache,
    value_cache,
    cache_lengths,
    visible,
):
    dma = pltpu.SemaphoreType.DMA
    hbm = pl.BlockSpec(memory_space=pl.ANY)
    smem = pl.BlockSpec(memory_space=pltpu.SMEM)
    vmem = pl.BlockSpec(memory_space=pltpu.VMEM)
    scratch = [
        pltpu.VMEM((CHIPS, GROUP, FEAT), BF16),
        pltpu.VMEM((1, FEAT), BF16),
        pltpu.VMEM((ALL, FEAT), BF16),
        pltpu.VMEM((FEAT, 1024), BF16),
        pltpu.VMEM((FEAT, 2 * HD), BF16),
        pltpu.VMEM((1024, FEAT), BF16),
        pltpu.VMEM((SLOTS, HD), BF16),
        pltpu.VMEM((HD, SLOTS), BF16),
        pltpu.VMEM((SLOTS, 2 * HD), BF16),
        pltpu.VMEM((HD, HD), BF16),
        pltpu.VMEM((HD, 2 * HD), BF16),
        pltpu.VMEM((CHIPS, FLAT, HD), F32),
        pltpu.VMEM((GROUP, HD), F32),
        pltpu.VMEM((PARTS, ALL, WIDE), F32),
        pltpu.VMEM((CHIPS, PROMPT_G, 2 * HD), F32),
        pltpu.VMEM((PARTS, ALL, WIDE), BF16),
        pltpu.VMEM((PARTS, ALL, WIDE), BF16),
        pltpu.VMEM((CHIPS, PROMPT_G, 2 * HD), BF16),
        pltpu.VMEM((CHIPS, PROMPT_G, 2 * HD), BF16),
        pltpu.VMEM((CHIPS, 1, HD), F32),
        pltpu.VMEM((CHIPS, 1, HD), F32),
        pltpu.VMEM((PARTS, CHIPS, GROUP, WIDE), BF16),
        pltpu.VMEM((PARTS, CHIPS, GROUP, WIDE), BF16),
        pltpu.VMEM((CHIPS, PROMPT_G, 2 * HD), BF16),
        pltpu.VMEM((CHIPS, PROMPT_G, 2 * HD), BF16),
        pltpu.VMEM((CHIPS, 1, HD), F32),
        pltpu.VMEM((CHIPS, 1, HD), F32),
        pltpu.VMEM((PARTS, 2, CHIPS, FLAT, HD), BF16),
        pltpu.VMEM((TILES, BLOCK, TILE), F32),
        pltpu.VMEM((BLOCK, HD), F32),
        pltpu.VMEM((BLOCK, HD), F32),
        pltpu.VMEM((PARTS, CHIPS, FLAT, HD), F32),
        pltpu.VMEM((PARTS, CHIPS, 8, HD), F32),
        pltpu.VMEM((PARTS, CHIPS, FLAT + 16, HD), BF16),
        pltpu.VMEM((PARTS, CHIPS, FLAT + 16, HD), BF16),
        pltpu.VMEM((PARTS, CHIPS, FLAT + 16, HD), BF16),
        pltpu.VMEM((PARTS, CHIPS, FLAT + 16, HD), BF16),
        pltpu.VMEM((PARTS, 2, CHIPS, GROUP, WIDE), BF16),
        pltpu.VMEM((ALL, FEAT), F32),
        pltpu.VMEM((KV, GROUP, FEAT), BF16),
        pltpu.VMEM((KV, GROUP, FEAT), BF16),
        dma((11,)),
        dma((2 * PARTS + 2,)),
        dma((2 * PARTS + 2,)),
        dma((PARTS, CHIPS)),
        dma((PARTS, CHIPS)),
        dma((CHIPS,)),
        dma((CHIPS,)),
        dma((CHIPS,)),
        dma((CHIPS,)),
        dma((PARTS, CHIPS)),
        dma((PARTS, CHIPS)),
        dma((PARTS, CHIPS)),
        dma((PARTS, CHIPS)),
        dma((PARTS, CHIPS)),
        dma((PARTS, CHIPS)),
        dma((PARTS, CHIPS)),
        dma((PARTS, CHIPS)),
        dma((PARTS, CHIPS)),
        dma((PARTS, CHIPS)),
        dma((KV,)),
        dma((KV,)),
    ]
    return pl.pallas_call(
        kernel,
        out_shape=(
            jax.ShapeDtypeStruct((PROMPT_G, FEAT), BF16),
            jax.ShapeDtypeStruct((STEPS, ROWS_G, FEAT), BF16),
        ),
        in_specs=[hbm] * 9 + [smem] * 2,
        out_specs=(vmem, vmem),
        scratch_shapes=scratch,
        compiler_params=pltpu.CompilerParams(
            collective_id=0, has_side_effects=True, vmem_limit_bytes=58 * 2**20
        ),
    )(
        prompt_in.reshape(CHIPS, PROMPT_G, FEAT),
        step_in.reshape(STEPS, CHIPS, ROWS_G, FEAT),
        norm_gain.reshape(1, FEAT),
        query_weight,
        key_weight,
        value_weight,
        out_weight,
        key_cache.reshape(SLOTS, HD),
        value_cache.reshape(SLOTS, HD),
        cache_lengths,
        visible,
    )


def solution(mesh):
    placed = (
        P(None, "ctx"),
        P(None, None, "ctx"),
        P("ctx"),
        P("ctx", "kv"),
        P("ctx", "kv"),
        P("ctx", "kv"),
        P("kv", "ctx"),
        P("kv", "ctx", None),
        P("kv", "ctx", None),
        P("ctx"),
        P(),
    )
    return jax.shard_map(
        on_device,
        mesh=mesh,
        in_specs=placed,
        out_specs=(P("kv", "ctx"), P(None, "kv", "ctx")),
        check_vma=False,
    )
```

```python
import jax
import jax.numpy as jnp
from jax import lax
from jax.experimental import pallas as pl
from jax.experimental.pallas import tpu as pltpu
from jax.sharding import PartitionSpec as P

D = 8192
HD = 128
EPSILON = 1e-05
MESH = pl.DeviceIdType.MESH
F32 = jnp.float32
BF16 = jnp.bfloat16

CTX = 16
KV = 8
CHIPS = 8
PROMPT = 256
ROWS = 64
STEPS = 3
PROMPT_N = PROMPT // ROWS
GRANULES = PROMPT_N + STEPS
SUB = ROWS // CHIPS
OWN = GRANULES * SUB
ALL = GRANULES * ROWS
FEAT = 512
WIDE = 512
HEADS = WIDE // HD
FLAT = HEADS * SUB
HALF = CHIPS * FLAT
BLOCK = 2 * HALF
PACK = FLAT + 8
SLOTS = 8192
TILE = 512
TILES = SLOTS // TILE
LOG2E = 1.4426950408889634
HIDDEN = -1e30
FRONT = ((0, 2), (2, 2), (4, 3))
BACK = ((0, 2), (2, 2), (4, 1), (5, 2))
DIRECT_Q = (False, True, False)
DIRECT_A = (False, False, False, False)


def kernel(
    prompt_ref,
    step_ref,
    gain_ref,
    wq_hbm,
    wk_hbm,
    wv_hbm,
    wo_hbm,
    key_hbm,
    value_hbm,
    length_ref,
    visible_ref,
    prompt_out,
    step_out,
    x_raw,
    gain,
    xs,
    wq,
    wkv,
    wo,
    k_raw,
    k_t,
    v_x,
    kx_t,
    vx_x,
    bias,
    inv,
    po,
    kvp,
    a0_send,
    a0_recv,
    kv0_send,
    kv0_recv,
    sq0_send,
    sq0_recv,
    a1_send,
    a1_recv,
    kv1_send,
    kv1_recv,
    sq1_send,
    sq1_recv,
    q_all,
    s_buf,
    sx_buf,
    mx,
    mix_all,
    top_all,
    b0_send,
    b0_recv,
    b1_send,
    b1_recv,
    att,
    cp_send,
    cp_recv,
    cs_send,
    cs_recv,
    load_sem,
    a0_ss,
    a0_rs,
    b0_ss,
    b0_rs,
    a1_ss,
    a1_rs,
    kv1_ss,
    kv1_rs,
    sq1_ss,
    sq1_rs,
    qg_ss,
    qg_rs,
    qf_ss,
    qf_rs,
    b1_ss,
    b1_rs,
    ag_ss,
    ag_rs,
    af_ss,
    af_rs,
    c_ss,
    c_rs,
):
    c = lax.axis_index("ctx")
    k = lax.axis_index("kv")
    core = lax.rem(c, 2)
    j = lax.div(c, 2)
    other = 1 - core
    sib = (c + 1 - 2 * core, k)
    any_direct = any(DIRECT_Q) or any(DIRECT_A)

    def chip(jt):
        return (2 * jt + core, k)

    def cross(jt):
        return (2 * jt + other, k)

    def away(d):
        return lax.rem(j + d, CHIPS)

    def remote(src, dst, ss, rs, dev):
        return pltpu.make_async_remote_copy(
            src_ref=src, dst_ref=dst, send_sem=ss, recv_sem=rs, device_id=dev, device_id_type=MESH
        )

    loads = [
        pltpu.make_async_copy(prompt_ref, x_raw.at[0:PROMPT], load_sem.at[0]),
        pltpu.make_async_copy(step_ref, x_raw.at[PROMPT:ALL], load_sem.at[1]),
        pltpu.make_async_copy(gain_ref, gain, load_sem.at[2]),
    ]
    weights_load = pltpu.make_async_copy(wq_hbm, wq, load_sem.at[3])
    pair_loads = [
        pltpu.make_async_copy(wk_hbm, wkv.at[:, 0:HD], load_sem.at[4]),
        pltpu.make_async_copy(wv_hbm, wkv.at[:, HD : 2 * HD], load_sem.at[5]),
    ]
    key_load = pltpu.make_async_copy(key_hbm, k_raw, load_sem.at[6])
    value_load = pltpu.make_async_copy(value_hbm, v_x.at[:, 0:HD], load_sem.at[7])
    wo_load = pltpu.make_async_copy(wo_hbm, wo, load_sem.at[8])
    for copy in loads:
        copy.start()
    weights_load.start()
    for copy in pair_loads:
        copy.start()

    barrier = pltpu.get_barrier_semaphore()
    pl.semaphore_signal(barrier, inc=1, device_id=sib, device_id_type=MESH)
    for d in range(1, CHIPS):
        pl.semaphore_signal(barrier, inc=1, device_id=chip(away(d)), device_id_type=MESH)
        if any_direct:
            pl.semaphore_signal(barrier, inc=1, device_id=cross(away(d)), device_id_type=MESH)
        pl.semaphore_signal(
            barrier, inc=1, device_id=(c, lax.rem(k + d, KV)), device_id_type=MESH
        )

    eye_flat = lax.broadcasted_iota(jnp.int32, (FLAT, HD), 0) == lax.broadcasted_iota(
        jnp.int32, (FLAT, HD), 1
    )
    eye_own = lax.broadcasted_iota(jnp.int32, (OWN, HD), 0) == lax.broadcasted_iota(
        jnp.int32, (OWN, HD), 1
    )

    def as_row(eye, column):
        return jnp.sum(jnp.where(eye, column, 0.0), axis=0, keepdims=True)

    def as_column(eye, row):
        return jnp.sum(jnp.where(eye, row, 0.0), axis=1, keepdims=True)

    for copy in loads:
        copy.wait()
    xf = x_raw[...].astype(F32)
    xs[...] = (xf * gain[...].astype(F32).reshape(1, FEAT)).astype(BF16)
    squares = jnp.sum(xf * xf, axis=1, keepdims=True)
    for jt in range(CHIPS):
        sq0_send[jt] = as_row(
            eye_own,
            jnp.concatenate(
                [squares[g * ROWS + jt * SUB : g * ROWS + (jt + 1) * SUB] for g in range(GRANULES)],
                axis=0,
            ),
        )
    weights_load.wait()
    for copy in pair_loads:
        copy.wait()
    key_load.start()
    value_load.start()
    wo_load.start()

    def rows_of(part):
        return slice(part[0] * ROWS, (part[0] + part[1]) * ROWS)

    def first(f):
        rows = rows_of(FRONT[f])
        return remote(a0_send.at[rows], a0_recv.at[rows], a0_ss.at[f], a0_rs.at[f], sib)

    def project(rows, column):
        return jnp.dot(
            xs[rows], wq[:, pl.ds(pl.multiple_of(column, HD), WIDE)], preferred_element_type=F32
        )

    kv_first = remote(kv0_send, kv0_recv, a0_ss.at[len(FRONT)], a0_rs.at[len(FRONT)], sib)
    sq_first = remote(sq0_send, sq0_recv, a0_ss.at[len(FRONT) + 1], a0_rs.at[len(FRONT) + 1], sib)
    start_rows = rows_of(FRONT[0])
    later_rows = slice(start_rows.stop, ALL)
    a0_send[start_rows] = project(start_rows, other * WIDE).astype(BF16)
    pl.semaphore_wait(barrier, (3 if any_direct else 2) * CHIPS - (2 if any_direct else 1))
    sq_first.start()
    first(0).start()
    po[start_rows] = project(start_rows, core * WIDE)

    length = length_ref[0]

    def prepare_keys(t, carry):
        low = pl.multiple_of(t * TILE, TILE)
        live = (lax.broadcasted_iota(jnp.int32, (TILE, HD), 0) + low) < length
        keys = jnp.where(live, k_raw[pl.ds(low, TILE)].astype(F32), k_raw[0:1].astype(F32))
        k_t[:, pl.ds(low, TILE)] = keys.astype(BF16).T
        return carry

    def prepare_values(t, carry):
        low = pl.multiple_of(t * TILE, TILE)
        live = (lax.broadcasted_iota(jnp.int32, (TILE, HD), 0) + low) < length
        v_x[pl.ds(low, TILE), 0:HD] = jnp.where(
            live, v_x[pl.ds(low, TILE), 0:HD].astype(F32), 0.0
        ).astype(BF16)
        v_x[pl.ds(low, TILE), HD : 2 * HD] = jnp.where(live, 1.0, 0.0).astype(BF16)
        return carry

    def span(part):
        return pl.ds(part[0], part[1])

    def a1_copy(f, jt, slot):
        grans = span(FRONT[f])
        return remote(
            a1_send.at[jt, grans],
            a1_recv.at[slot, grans],
            a1_ss.at[f, jt],
            a1_rs.at[f, slot],
            chip(jt),
        )

    def kv1_copy(jt, slot):
        return remote(kv1_send.at[jt], kv1_recv.at[slot], kv1_ss.at[jt], kv1_rs.at[slot], chip(jt))

    def sq1_copy(jt, slot):
        return remote(sq1_send.at[jt], sq1_recv.at[slot], sq1_ss.at[jt], sq1_rs.at[slot], chip(jt))

    def spread(f):
        first(f).wait_recv()
        g0, count = FRONT[f]
        for g in range(g0, g0 + count):
            rows = slice(g * ROWS, (g + 1) * ROWS)
            total = po[rows] + a0_recv[rows].astype(F32)
            a1_send[:, g] = total.reshape(CHIPS, SUB, WIDE).astype(BF16)
        for d in range(1, CHIPS):
            a1_copy(f, away(d), j).start()

    def spread_squares():
        sq_first.wait_recv()
        sq1_send[...] = sq0_send[...] + sq0_recv[...]
        for d in range(1, CHIPS):
            sq1_copy(away(d), j).start()

    def spread_pairs():
        kv_first.wait_recv()
        kv1_send[...] = (kvp[...] + kv0_recv[...].astype(F32)).astype(BF16)
        for d in range(1, CHIPS):
            kv1_copy(away(d), j).start()

    def square_sums():
        square = sq1_send[j]
        for d in range(1, CHIPS):
            src = away(d)
            sq1_copy(src, src).wait_recv()
            square = square + sq1_recv[src]
        inverse = lax.rsqrt(square / D + EPSILON)
        inv[...] = jnp.broadcast_to(as_column(eye_own, inverse), (OWN, HD))

    def pair_sums():
        pair = kv1_send[j].astype(F32)
        for d in range(1, CHIPS):
            src = away(d)
            kv1_copy(src, src).wait_recv()
            pair = pair + kv1_recv[src].astype(F32)
        pair = pair.reshape(PROMPT_N * SUB, 2 * HD)
        split = PROMPT_N * SUB
        inv_steps = jnp.concatenate([inv[split:], jnp.zeros((2 * split - OWN, HD), F32)], axis=0)
        scale = jnp.where(core == 0, inv[0:split], inv_steps)
        blank = jnp.zeros((HD - split, HD), F32)
        new_keys = jnp.concatenate([pair[:, 0:HD] * scale, blank], axis=0)
        new_values = jnp.concatenate([pair[:, HD:] * scale, blank], axis=0)
        kx_t[...] = new_keys.T.astype(BF16)
        vx_x[:, 0:HD] = new_values.astype(BF16)
        vx_x[:, HD : 2 * HD] = jnp.ones((HD, HD), BF16)

    def q_at(f, column, slot):
        return q_all.at[span(FRONT[f]), column, slot]

    def q_copy(f, jt, slot):
        return remote(
            q_at(f, core, slot), q_at(f, core, slot), qg_ss.at[f, jt], qg_rs.at[f, slot], chip(jt)
        )

    def q_cross(f, jt):
        return remote(
            q_at(f, core, j), q_at(f, core, j), qf_ss.at[f, jt], qf_rs.at[f, j], cross(jt)
        )

    def q_forward(f, column, slot):
        return remote(
            q_at(f, column, slot), q_at(f, column, slot), qf_ss.at[f, slot], qf_rs.at[f, slot], sib
        )

    def query_sums(f):
        g0, count = FRONT[f]
        grans = span(FRONT[f])
        total = a1_send[j, grans].astype(F32)
        for d in range(1, CHIPS):
            src = away(d)
            a1_copy(f, src, src).wait_recv()
            total = total + a1_recv[src, grans].astype(F32)
        for i in range(count):
            g = g0 + i
            scale = inv[g * SUB : (g + 1) * SUB] * (HD**-0.5 * LOG2E)
            flat = jnp.concatenate(
                [total[i, :, h * HD : (h + 1) * HD] * scale for h in range(HEADS)], axis=0
            )
            q_all[g, core, j] = flat.astype(BF16)
        for d in range(1, CHIPS):
            q_copy(f, away(d), j).start()
            if DIRECT_Q[f]:
                q_cross(f, away(d)).start()
        q_forward(f, core, j).start()

    def forward_queries(f):
        for d in range(1, CHIPS):
            src = away(d)
            q_copy(f, src, src).wait_recv()
            if not DIRECT_Q[f]:
                q_forward(f, core, src).start()

    def await_queries(f):
        for slot in range(CHIPS):
            q_forward(f, other, slot).wait_recv()

    def prepare_bias():
        lane = lax.broadcasted_iota(jnp.int32, (SUB, HD), 1)
        sub = lax.broadcasted_iota(jnp.int32, (SUB, HD), 0)
        lane_sub = lax.rem(lane, SUB)
        lane_gran = lax.div(lane, SUB)
        position = lane_gran * ROWS + j * SUB + lane_sub
        key_row = j * SUB + lane_sub
        for jt in range(CHIPS):
            seen_by_row = jnp.zeros((SUB, HD), jnp.int32)
            for b in range(SUB):
                seen_by_row = jnp.where(sub == b, visible_ref[jt * SUB + b], seen_by_row)
            query_row = jt * SUB + sub
            for g in range(GRANULES):
                limit = g * ROWS + query_row + 1 if g < PROMPT_N else seen_by_row
                on_prompt = jnp.where((lane_gran < PROMPT_N) & (position < limit), 0.0, HIDDEN)
                if g < PROMPT_N:
                    on_steps = jnp.full((SUB, HD), HIDDEN, F32)
                else:
                    on_steps = jnp.where(
                        (lane_gran <= g - PROMPT_N) & (key_row == query_row), 0.0, HIDDEN
                    )
                bias[g, jt] = jnp.where(core == 0, on_prompt, on_steps)

    key_load.wait()
    lax.fori_loop(0, TILES // 4, prepare_keys, 0)
    spread(0)
    spread_squares()
    a0_send[later_rows] = project(later_rows, other * WIDE).astype(BF16)
    for f in range(1, len(FRONT)):
        first(f).start()
    pairs = jnp.dot(xs[...], wkv[...], preferred_element_type=F32)
    pairs = pairs.reshape(GRANULES, CHIPS, SUB, 2 * HD)
    for i in range(PROMPT_N):
        of_prompt = pairs[i]
        of_steps = pairs[PROMPT_N + i] if i < STEPS else jnp.zeros((CHIPS, SUB, 2 * HD), F32)
        kv0_send[:, i] = jnp.where(core == 0, of_steps, of_prompt).astype(BF16)
        kvp[:, i] = jnp.where(core == 0, of_prompt, of_steps)
    kv_first.start()
    po[later_rows] = project(later_rows, core * WIDE)
    spread_pairs()
    square_sums()
    query_sums(0)
    spread(1)
    prepare_bias()
    lax.fori_loop(TILES // 4, TILES, prepare_keys, 0)
    forward_queries(0)
    query_sums(1)
    spread(2)
    value_load.wait()
    lax.fori_loop(0, TILES, prepare_values, 0)
    pair_sums()
    await_queries(0)

    def lane_max(scores):
        high = scores[:, 0:HD]
        for u in range(1, scores.shape[1] // HD):
            high = jnp.maximum(high, scores[:, u * HD : (u + 1) * HD])
        return high

    def sweep(n_scores, top):
        if n_scores is not None:
            queries = q_all[n_scores].reshape(BLOCK, HD)
            mask = bias[n_scores].reshape(1, CHIPS, 1, SUB, HD)
        high = None
        mixed = None
        for t in range(TILES + 1):
            cols = slice(t * TILE, (t + 1) * TILE)
            if top is not None:
                old = s_buf[t] if t < TILES else sx_buf[...]
                weights = jnp.exp2(old - top).astype(BF16)
            if n_scores is not None:
                if t < TILES:
                    scores = jnp.dot(queries, k_t[:, cols], preferred_element_type=F32)
                    s_buf[t] = scores
                else:
                    scores = jnp.dot(queries, kx_t[...], preferred_element_type=F32)
                    scores = scores.reshape(2, CHIPS, HEADS, SUB, HD) + mask
                    scores = scores.reshape(BLOCK, HD)
                    sx_buf[...] = scores
                peak = lane_max(scores)
                high = peak if high is None else jnp.maximum(high, peak)
            if top is not None:
                values = v_x[cols] if t < TILES else vx_x[...]
                part = jnp.dot(weights, values, preferred_element_type=F32)
                mixed = part if mixed is None else mixed + part
        if n_scores is not None:
            mx[...] = high
        return mixed

    def split3(row):
        one = row.astype(BF16).astype(F32)
        two = (row - one).astype(BF16).astype(F32)
        return one, two, row - one - two

    def packed(mixture, top_row, total_row):
        sub = lax.broadcasted_iota(jnp.int32, (PACK - FLAT, HD), 0)
        stats = jnp.zeros((PACK - FLAT, HD), F32)
        for i, piece in enumerate(split3(top_row) + split3(total_row)):
            stats = jnp.where(sub == i, piece, stats)
        return jnp.concatenate([mixture, stats], axis=0).astype(BF16)

    def unpacked(packet):
        wide = packet.astype(F32)
        stats = wide[FLAT:]
        return (
            wide[0:FLAT],
            stats[0:1] + stats[1:2] + stats[2:3],
            stats[3:4] + stats[4:5] + stats[5:6],
        )

    def block_of(n, column, jt):
        rows = slice(jt * FLAT, (jt + 1) * FLAT)
        top_row = as_row(eye_flat, top_all[n, column, rows])
        total_row = as_row(eye_flat, mix_all[n, column, rows, HD:])
        return mix_all[n, column, rows, 0:HD], top_row, total_row

    def keep(n, mixed, top):
        mix_all[n] = mixed.reshape(2, HALF, 2 * HD)
        top_all[n] = jnp.broadcast_to(top, (BLOCK, HD)).reshape(2, HALF, HD)
        for jt in range(CHIPS):
            b0_send[n, jt] = packed(*block_of(n, other, jt))

    def b0_copy(b):
        grans = span(BACK[b])
        return remote(b0_send.at[grans], b0_recv.at[grans], b0_ss.at[b], b0_rs.at[b], sib)

    def b1_copy(b, jt, slot):
        grans = span(BACK[b])
        return remote(
            b1_send.at[jt, grans], b1_recv.at[slot, grans], b1_ss.at[b, jt], b1_rs.at[b, slot], chip(jt)
        )

    def merge_pair(b):
        b0_copy(b).wait_recv()
        g0, count = BACK[b]
        for g in range(g0, g0 + count):
            for jt in range(CHIPS):
                mix1, top1, tot1 = unpacked(b0_recv[g, jt])
                mix0, top0, tot0 = block_of(g, core, jt)
                top = jnp.maximum(top0, top1)
                w0 = jnp.exp2(top0 - top)
                w1 = jnp.exp2(top1 - top)
                mixture = mix0 * as_column(eye_flat, w0) + mix1 * as_column(eye_flat, w1)
                b1_send[jt, g] = packed(mixture, top, w0 * tot0 + w1 * tot1)
        for d in range(1, CHIPS):
            b1_copy(b, away(d), j).start()

    def att_at(b, column, slot):
        return att.at[column, span(BACK[b]), slot]

    def att_copy(b, jt, slot):
        return remote(
            att_at(b, core, slot), att_at(b, core, slot), ag_ss.at[b, jt], ag_rs.at[b, slot], chip(jt)
        )

    def att_cross(b, jt):
        return remote(
            att_at(b, core, j), att_at(b, core, j), af_ss.at[b, jt], af_rs.at[b, j], cross(jt)
        )

    def att_forward(b, column, slot):
        return remote(
            att_at(b, column, slot),
            att_at(b, column, slot),
            af_ss.at[b, slot],
            af_rs.at[b, slot],
            sib,
        )

    def merge_all(b):
        g0, count = BACK[b]
        for d in range(1, CHIPS):
            b1_copy(b, away(d), away(d)).wait_recv()
        for g in range(g0, g0 + count):
            pieces = [unpacked(b1_send[j, g])]
            for d in range(1, CHIPS):
                pieces.append(unpacked(b1_recv[away(d), g]))
            top = pieces[0][1]
            for piece in pieces[1:]:
                top = jnp.maximum(top, piece[1])
            shares = [jnp.exp2(piece[1] - top) for piece in pieces]
            total = shares[0] * pieces[0][2]
            for share, piece in zip(shares[1:], pieces[1:]):
                total = total + share * piece[2]
            result = jnp.zeros((FLAT, HD), F32)
            for share, piece in zip(shares, pieces):
                result = result + piece[0] * as_column(eye_flat, share)
            result = result * as_column(eye_flat, 1.0 / total)
            att[core, g, j] = jnp.concatenate(
                [result[h * SUB : (h + 1) * SUB] for h in range(HEADS)], axis=1
            ).astype(BF16)
        for d in range(1, CHIPS):
            att_copy(b, away(d), j).start()
            if DIRECT_A[b]:
                att_cross(b, away(d)).start()
        att_forward(b, core, j).start()

    def forward_attended(b):
        for d in range(1, CHIPS):
            src = away(d)
            att_copy(b, src, src).wait_recv()
            if not DIRECT_A[b]:
                att_forward(b, core, src).start()

    def await_attended(b):
        for slot in range(CHIPS):
            att_forward(b, other, slot).wait_recv()

    def out_part(g0, count, column):
        rows = att[column, g0 : g0 + count].astype(F32).reshape(count * ROWS, WIDE).astype(BF16)
        low = pl.multiple_of(column * WIDE, WIDE)
        return jnp.dot(rows, wo[pl.ds(low, WIDE)], preferred_element_type=F32)

    def cp_copy(kt, slot):
        return remote(cp_send.at[kt], cp_recv.at[slot], c_ss.at[0, kt], c_rs.at[0, slot], (c, kt))

    def cs_copy(kt, slot):
        return remote(cs_send.at[kt], cs_recv.at[slot], c_ss.at[1, kt], c_rs.at[1, slot], (c, kt))

    def next_kv(d):
        return lax.rem(k + d, KV)

    def finish_prompt():
        result = out_part(0, PROMPT_N, core) + out_part(0, PROMPT_N, other)
        cp_send[...] = result.reshape(KV, PROMPT // KV, FEAT).astype(BF16)
        for d in range(1, KV):
            cp_copy(next_kv(d), k).start()

    def finish_steps():
        result = out_part(PROMPT_N, STEPS, core) + out_part(PROMPT_N, STEPS, other)
        for s in range(STEPS):
            piece = result[s * ROWS : (s + 1) * ROWS]
            cs_send[:, s] = piece.reshape(KV, SUB, FEAT).astype(BF16)
        for d in range(1, KV):
            cs_copy(next_kv(d), k).start()

    def write_prompt():
        final = cp_send[k].astype(F32)
        for d in range(1, KV):
            src = next_kv(d)
            cp_copy(src, src).wait_recv()
            final = final + cp_recv[src].astype(F32)
        prompt_out[...] = final.astype(BF16)

    def write_steps():
        final = cs_send[k].astype(F32)
        for d in range(1, KV):
            src = next_kv(d)
            cs_copy(src, src).wait_recv()
            final = final + cs_recv[src].astype(F32)
        step_out[...] = final.astype(BF16)

    def step_top():
        return jnp.max(mx[...], axis=1, keepdims=True)

    sweep(0, None)

    def step(n, carry):
        @pl.when(n == 1)
        def _():
            forward_queries(1)
            query_sums(2)
            await_queries(1)

        @pl.when(n == 2)
        def _():
            b0_copy(0).start()
            forward_queries(2)

        @pl.when(n == 3)
        def _():
            await_queries(2)
            merge_pair(0)

        @pl.when(n == 4)
        def _():
            b0_copy(1).start()
            merge_all(0)

        @pl.when(n == 5)
        def _():
            b0_copy(2).start()
            merge_pair(1)
            forward_attended(0)

        top = step_top()
        keep(n, sweep(n + 1, top), top)
        return carry

    last = GRANULES - 1
    lax.fori_loop(0, last, step, 0)
    merge_pair(2)
    merge_all(1)
    top = step_top()
    keep(last, sweep(None, top), top)
    b0_copy(3).start()
    merge_all(2)
    forward_attended(1)
    merge_pair(3)
    await_attended(0)
    await_attended(1)
    wo_load.wait()
    finish_prompt()
    forward_attended(2)
    merge_all(3)
    forward_attended(3)
    write_prompt()
    await_attended(2)
    await_attended(3)
    finish_steps()
    write_steps()

    kv_first.wait_send()
    sq_first.wait_send()
    for f in range(len(FRONT)):
        first(f).wait_send()
        q_forward(f, core, j).wait_send()
    for b in range(len(BACK)):
        b0_copy(b).wait_send()
        att_forward(b, core, j).wait_send()
    for d in range(1, CHIPS):
        jt = away(d)
        sq1_copy(jt, j).wait_send()
        kv1_copy(jt, j).wait_send()
        cp_copy(next_kv(d), k).wait_send()
        cs_copy(next_kv(d), k).wait_send()
        for f in range(len(FRONT)):
            a1_copy(f, jt, j).wait_send()
            q_copy(f, jt, j).wait_send()
            if DIRECT_Q[f]:
                q_cross(f, jt).wait_send()
            else:
                q_forward(f, core, jt).wait_send()
        for b in range(len(BACK)):
            b1_copy(b, jt, j).wait_send()
            att_copy(b, jt, j).wait_send()
            if DIRECT_A[b]:
                att_cross(b, jt).wait_send()
            else:
                att_forward(b, core, jt).wait_send()


def place_outputs(prompt_ref, step_ref, prompt_out, step_out):
    prompt_out[...] = prompt_ref[...]
    step_out[...] = step_ref[...]


def on_device(
    prompt_in,
    step_in,
    norm_gain,
    query_weight,
    key_weight,
    value_weight,
    out_weight,
    key_cache,
    value_cache,
    cache_lengths,
    visible,
):
    dma = pltpu.SemaphoreType.DMA
    hbm = pl.BlockSpec(memory_space=pl.ANY)
    smem = pl.BlockSpec(memory_space=pltpu.SMEM)
    vmem = pl.BlockSpec(memory_space=pltpu.VMEM)
    fronts, backs = len(FRONT), len(BACK)
    scratch = [
        pltpu.VMEM((ALL, FEAT), BF16),
        pltpu.VMEM((FEAT,), BF16),
        pltpu.VMEM((ALL, FEAT), BF16),
        pltpu.VMEM((FEAT, 2 * WIDE), BF16),
        pltpu.VMEM((FEAT, 2 * HD), BF16),
        pltpu.VMEM((2 * WIDE, FEAT), BF16),
        pltpu.VMEM((SLOTS, HD), BF16),
        pltpu.VMEM((HD, SLOTS), BF16),
        pltpu.VMEM((SLOTS, 2 * HD), BF16),
        pltpu.VMEM((HD, HD), BF16),
        pltpu.VMEM((HD, 2 * HD), BF16),
        pltpu.VMEM((GRANULES, CHIPS, SUB, HD), F32),
        pltpu.VMEM((OWN, HD), F32),
        pltpu.VMEM((ALL, WIDE), F32),
        pltpu.VMEM((CHIPS, PROMPT_N, SUB, 2 * HD), F32),
        pltpu.VMEM((ALL, WIDE), BF16),
        pltpu.VMEM((ALL, WIDE), BF16),
        pltpu.VMEM((CHIPS, PROMPT_N, SUB, 2 * HD), BF16),
        pltpu.VMEM((CHIPS, PROMPT_N, SUB, 2 * HD), BF16),
        pltpu.VMEM((CHIPS, 1, HD), F32),
        pltpu.VMEM((CHIPS, 1, HD), F32),
        pltpu.VMEM((CHIPS, GRANULES, SUB, WIDE), BF16),
        pltpu.VMEM((CHIPS, GRANULES, SUB, WIDE), BF16),
        pltpu.VMEM((CHIPS, PROMPT_N, SUB, 2 * HD), BF16),
        pltpu.VMEM((CHIPS, PROMPT_N, SUB, 2 * HD), BF16),
        pltpu.VMEM((CHIPS, 1, HD), F32),
        pltpu.VMEM((CHIPS, 1, HD), F32),
        pltpu.VMEM((GRANULES, 2, CHIPS, FLAT, HD), BF16),
        pltpu.VMEM((TILES, BLOCK, TILE), F32),
        pltpu.VMEM((BLOCK, HD), F32),
        pltpu.VMEM((BLOCK, HD), F32),
        pltpu.VMEM((GRANULES, 2, HALF, 2 * HD), F32),
        pltpu.VMEM((GRANULES, 2, HALF, HD), F32),
        pltpu.VMEM((GRANULES, CHIPS, PACK, HD), BF16),
        pltpu.VMEM((GRANULES, CHIPS, PACK, HD), BF16),
        pltpu.VMEM((CHIPS, GRANULES, PACK, HD), BF16),
        pltpu.VMEM((CHIPS, GRANULES, PACK, HD), BF16),
        pltpu.VMEM((2, GRANULES, CHIPS, SUB, WIDE), BF16),
        pltpu.VMEM((KV, PROMPT // KV, FEAT), BF16),
        pltpu.VMEM((KV, PROMPT // KV, FEAT), BF16),
        pltpu.VMEM((KV, STEPS, SUB, FEAT), BF16),
        pltpu.VMEM((KV, STEPS, SUB, FEAT), BF16),
        dma((9,)),
        dma((fronts + 2,)),
        dma((fronts + 2,)),
        dma((backs,)),
        dma((backs,)),
        dma((fronts, CHIPS)),
        dma((fronts, CHIPS)),
        dma((CHIPS,)),
        dma((CHIPS,)),
        dma((CHIPS,)),
        dma((CHIPS,)),
        dma((fronts, CHIPS)),
        dma((fronts, CHIPS)),
        dma((fronts, CHIPS)),
        dma((fronts, CHIPS)),
        dma((backs, CHIPS)),
        dma((backs, CHIPS)),
        dma((backs, CHIPS)),
        dma((backs, CHIPS)),
        dma((backs, CHIPS)),
        dma((backs, CHIPS)),
        dma((2, KV)),
        dma((2, KV)),
    ]
    shapes = (
        jax.ShapeDtypeStruct((PROMPT // KV, FEAT), BF16),
        jax.ShapeDtypeStruct((STEPS, SUB, FEAT), BF16),
    )
    results = pl.pallas_call(
        kernel,
        out_shape=shapes,
        in_specs=[hbm] * 9 + [smem] * 2,
        out_specs=(vmem, vmem),
        scratch_shapes=scratch,
        compiler_params=pltpu.CompilerParams(
            collective_id=0, has_side_effects=True, vmem_limit_bytes=58 * 2**20
        ),
    )(
        prompt_in,
        step_in.reshape(STEPS * ROWS, FEAT),
        norm_gain,
        query_weight,
        key_weight,
        value_weight,
        out_weight,
        key_cache.reshape(SLOTS, HD),
        value_cache.reshape(SLOTS, HD),
        cache_lengths,
        visible,
    )
    return pl.pallas_call(
        place_outputs, out_shape=shapes, in_specs=[vmem] * 2, out_specs=(vmem, vmem)
    )(*results)


def solution(mesh):
    placed = (
        P(None, "ctx"),
        P(None, None, "ctx"),
        P("ctx"),
        P("ctx", "kv"),
        P("ctx", "kv"),
        P("ctx", "kv"),
        P("kv", "ctx"),
        P("kv", "ctx", None),
        P("kv", "ctx", None),
        P("ctx"),
        P(),
    )
    return jax.shard_map(
        on_device,
        mesh=mesh,
        in_specs=placed,
        out_specs=(P("kv", "ctx"), P(None, "kv", "ctx")),
        check_vma=False,
    )
```

```python
import jax
import jax.numpy as jnp
from jax import lax
from jax.experimental import pallas as pl
from jax.experimental.pallas import tpu as pltpu
from jax.sharding import PartitionSpec as P

D = 8192
HD = 128
EPSILON = 1e-05
MESH = pl.DeviceIdType.MESH
F32 = jnp.float32
BF16 = jnp.bfloat16

CTX = 16
KV = 8
CHIPS = 8
PROMPT = 256
ROWS = 64
STEPS = 3
PROMPT_N = PROMPT // ROWS
GRANULES = PROMPT_N + STEPS
SUB = ROWS // CHIPS
OWN = GRANULES * SUB
ALL = GRANULES * ROWS
FEAT = 512
WIDE = 512
HEADS = WIDE // HD
FLAT = HEADS * SUB
HALF = CHIPS * FLAT
BLOCK = 2 * HALF
PACK = FLAT + 8
SLOTS = 8192
TILE = 512
TILES = SLOTS // TILE
LOG2E = 1.4426950408889634
HIDDEN = -1e30
FRONT = ((0, 2), (2, 2), (4, 3))
BACK = ((0, 2), (2, 2), (4, 1), (5, 1), (6, 1))
DIRECT_Q = (False, False, False)
DIRECT_A = (False, False, False, False, False)


def kernel(
    prompt_ref,
    step_ref,
    gain_ref,
    wq_hbm,
    wk_hbm,
    wv_hbm,
    wo_hbm,
    key_hbm,
    value_hbm,
    length_ref,
    visible_ref,
    prompt_out,
    step_out,
    x_raw,
    gain,
    xs,
    wq,
    wkv,
    wo,
    k_raw,
    k_t,
    v_x,
    kx_t,
    vx_x,
    bias,
    inv,
    po,
    kvp,
    a0_send,
    a0_recv,
    kv0_send,
    kv0_recv,
    sq0_send,
    sq0_recv,
    a1_send,
    a1_recv,
    kv1_send,
    kv1_recv,
    sq1_send,
    sq1_recv,
    q_all,
    s_buf,
    sx_buf,
    mx,
    mix_all,
    top_all,
    b0_send,
    b0_recv,
    b1_send,
    b1_recv,
    att,
    cp_send,
    cp_recv,
    cs_send,
    cs_recv,
    load_sem,
    a0_ss,
    a0_rs,
    b0_ss,
    b0_rs,
    a1_ss,
    a1_rs,
    kv1_ss,
    kv1_rs,
    sq1_ss,
    sq1_rs,
    qg_ss,
    qg_rs,
    qf_ss,
    qf_rs,
    b1_ss,
    b1_rs,
    ag_ss,
    ag_rs,
    af_ss,
    af_rs,
    c_ss,
    c_rs,
):
    c = lax.axis_index("ctx")
    k = lax.axis_index("kv")
    core = lax.rem(c, 2)
    j = lax.div(c, 2)
    other = 1 - core
    sib = (c + 1 - 2 * core, k)
    any_direct = any(DIRECT_Q) or any(DIRECT_A)

    def chip(jt):
        return (2 * jt + core, k)

    def cross(jt):
        return (2 * jt + other, k)

    def away(d):
        return lax.rem(j + d, CHIPS)

    def remote(src, dst, ss, rs, dev):
        return pltpu.make_async_remote_copy(
            src_ref=src, dst_ref=dst, send_sem=ss, recv_sem=rs, device_id=dev, device_id_type=MESH
        )

    loads = [
        pltpu.make_async_copy(prompt_ref, x_raw.at[0:PROMPT], load_sem.at[0]),
        pltpu.make_async_copy(step_ref, x_raw.at[PROMPT:ALL], load_sem.at[1]),
        pltpu.make_async_copy(gain_ref, gain, load_sem.at[2]),
    ]
    weights_load = pltpu.make_async_copy(wq_hbm, wq, load_sem.at[3])
    pair_loads = [
        pltpu.make_async_copy(wk_hbm, wkv.at[:, 0:HD], load_sem.at[4]),
        pltpu.make_async_copy(wv_hbm, wkv.at[:, HD : 2 * HD], load_sem.at[5]),
    ]
    key_load = pltpu.make_async_copy(key_hbm, k_raw, load_sem.at[6])
    value_load = pltpu.make_async_copy(value_hbm, v_x.at[:, 0:HD], load_sem.at[7])
    wo_load = pltpu.make_async_copy(wo_hbm, wo, load_sem.at[8])
    for copy in loads:
        copy.start()
    weights_load.start()
    for copy in pair_loads:
        copy.start()

    barrier = pltpu.get_barrier_semaphore()
    pl.semaphore_signal(barrier, inc=1, device_id=sib, device_id_type=MESH)
    for d in range(1, CHIPS):
        pl.semaphore_signal(barrier, inc=1, device_id=chip(away(d)), device_id_type=MESH)
        if any_direct:
            pl.semaphore_signal(barrier, inc=1, device_id=cross(away(d)), device_id_type=MESH)
        pl.semaphore_signal(
            barrier, inc=1, device_id=(c, lax.rem(k + d, KV)), device_id_type=MESH
        )

    eye_flat = lax.broadcasted_iota(jnp.int32, (FLAT, HD), 0) == lax.broadcasted_iota(
        jnp.int32, (FLAT, HD), 1
    )
    eye_own = lax.broadcasted_iota(jnp.int32, (OWN, HD), 0) == lax.broadcasted_iota(
        jnp.int32, (OWN, HD), 1
    )

    def as_row(eye, column):
        return jnp.sum(jnp.where(eye, column, 0.0), axis=0, keepdims=True)

    def as_column(eye, row):
        return jnp.sum(jnp.where(eye, row, 0.0), axis=1, keepdims=True)

    for copy in loads:
        copy.wait()
    xf = x_raw[...].astype(F32)
    xs[...] = (xf * gain[...].astype(F32).reshape(1, FEAT)).astype(BF16)
    squares = jnp.sum(xf * xf, axis=1, keepdims=True)
    for jt in range(CHIPS):
        sq0_send[jt] = as_row(
            eye_own,
            jnp.concatenate(
                [squares[g * ROWS + jt * SUB : g * ROWS + (jt + 1) * SUB] for g in range(GRANULES)],
                axis=0,
            ),
        )
    weights_load.wait()
    for copy in pair_loads:
        copy.wait()
    key_load.start()
    value_load.start()
    wo_load.start()

    def rows_of(part):
        return slice(part[0] * ROWS, (part[0] + part[1]) * ROWS)

    def first(f):
        rows = rows_of(FRONT[f])
        return remote(a0_send.at[rows], a0_recv.at[rows], a0_ss.at[f], a0_rs.at[f], sib)

    def project(rows, column):
        return jnp.dot(
            xs[rows], wq[:, pl.ds(pl.multiple_of(column, HD), WIDE)], preferred_element_type=F32
        )

    kv_first = remote(kv0_send, kv0_recv, a0_ss.at[len(FRONT)], a0_rs.at[len(FRONT)], sib)
    sq_first = remote(sq0_send, sq0_recv, a0_ss.at[len(FRONT) + 1], a0_rs.at[len(FRONT) + 1], sib)
    start_rows = rows_of(FRONT[0])
    later_rows = slice(start_rows.stop, ALL)
    a0_send[start_rows] = project(start_rows, other * WIDE).astype(BF16)
    pl.semaphore_wait(barrier, (3 if any_direct else 2) * CHIPS - (2 if any_direct else 1))
    sq_first.start()
    first(0).start()
    po[start_rows] = project(start_rows, core * WIDE)

    length = length_ref[0]

    def prepare_keys(t, carry):
        low = pl.multiple_of(t * TILE, TILE)
        live = (lax.broadcasted_iota(jnp.int32, (TILE, HD), 0) + low) < length
        keys = jnp.where(live, k_raw[pl.ds(low, TILE)].astype(F32), k_raw[0:1].astype(F32))
        k_t[:, pl.ds(low, TILE)] = keys.astype(BF16).T
        return carry

    def prepare_values(t, carry):
        low = pl.multiple_of(t * TILE, TILE)
        live = (lax.broadcasted_iota(jnp.int32, (TILE, HD), 0) + low) < length
        v_x[pl.ds(low, TILE), 0:HD] = jnp.where(
            live, v_x[pl.ds(low, TILE), 0:HD].astype(F32), 0.0
        ).astype(BF16)
        v_x[pl.ds(low, TILE), HD : 2 * HD] = jnp.where(live, 1.0, 0.0).astype(BF16)
        return carry

    def span(part):
        return pl.ds(part[0], part[1])

    def a1_copy(f, jt, slot):
        grans = span(FRONT[f])
        return remote(
            a1_send.at[jt, grans],
            a1_recv.at[slot, grans],
            a1_ss.at[f, jt],
            a1_rs.at[f, slot],
            chip(jt),
        )

    def kv1_copy(jt, slot):
        return remote(kv1_send.at[jt], kv1_recv.at[slot], kv1_ss.at[jt], kv1_rs.at[slot], chip(jt))

    def sq1_copy(jt, slot):
        return remote(sq1_send.at[jt], sq1_recv.at[slot], sq1_ss.at[jt], sq1_rs.at[slot], chip(jt))

    def spread(f):
        first(f).wait_recv()
        g0, count = FRONT[f]
        for g in range(g0, g0 + count):
            rows = slice(g * ROWS, (g + 1) * ROWS)
            total = po[rows] + a0_recv[rows].astype(F32)
            a1_send[:, g] = total.reshape(CHIPS, SUB, WIDE).astype(BF16)
        for d in range(1, CHIPS):
            a1_copy(f, away(d), j).start()

    def spread_squares():
        sq_first.wait_recv()
        sq1_send[...] = sq0_send[...] + sq0_recv[...]
        for d in range(1, CHIPS):
            sq1_copy(away(d), j).start()

    def spread_pairs():
        kv_first.wait_recv()
        kv1_send[...] = (kvp[...] + kv0_recv[...].astype(F32)).astype(BF16)
        for d in range(1, CHIPS):
            kv1_copy(away(d), j).start()

    def square_sums():
        square = sq1_send[j]
        for d in range(1, CHIPS):
            src = away(d)
            sq1_copy(src, src).wait_recv()
            square = square + sq1_recv[src]
        inverse = lax.rsqrt(square / D + EPSILON)
        inv[...] = jnp.broadcast_to(as_column(eye_own, inverse), (OWN, HD))

    def pair_sums():
        pair = kv1_send[j].astype(F32)
        for d in range(1, CHIPS):
            src = away(d)
            kv1_copy(src, src).wait_recv()
            pair = pair + kv1_recv[src].astype(F32)
        pair = pair.reshape(PROMPT_N * SUB, 2 * HD)
        split = PROMPT_N * SUB
        inv_steps = jnp.concatenate([inv[split:], jnp.zeros((2 * split - OWN, HD), F32)], axis=0)
        scale = jnp.where(core == 0, inv[0:split], inv_steps)
        blank = jnp.zeros((HD - split, HD), F32)
        new_keys = jnp.concatenate([pair[:, 0:HD] * scale, blank], axis=0)
        new_values = jnp.concatenate([pair[:, HD:] * scale, blank], axis=0)
        kx_t[...] = new_keys.T.astype(BF16)
        vx_x[:, 0:HD] = new_values.astype(BF16)
        vx_x[:, HD : 2 * HD] = jnp.ones((HD, HD), BF16)

    def q_at(f, column, slot):
        return q_all.at[span(FRONT[f]), column, slot]

    def q_copy(f, jt, slot):
        return remote(
            q_at(f, core, slot), q_at(f, core, slot), qg_ss.at[f, jt], qg_rs.at[f, slot], chip(jt)
        )

    def q_cross(f, jt):
        return remote(
            q_at(f, core, j), q_at(f, core, j), qf_ss.at[f, jt], qf_rs.at[f, j], cross(jt)
        )

    def q_forward(f, column, slot):
        return remote(
            q_at(f, column, slot), q_at(f, column, slot), qf_ss.at[f, slot], qf_rs.at[f, slot], sib
        )

    def query_sums(f):
        g0, count = FRONT[f]
        grans = span(FRONT[f])
        total = a1_send[j, grans].astype(F32)
        for d in range(1, CHIPS):
            src = away(d)
            a1_copy(f, src, src).wait_recv()
            total = total + a1_recv[src, grans].astype(F32)
        for i in range(count):
            g = g0 + i
            scale = inv[g * SUB : (g + 1) * SUB] * (HD**-0.5 * LOG2E)
            flat = jnp.concatenate(
                [total[i, :, h * HD : (h + 1) * HD] * scale for h in range(HEADS)], axis=0
            )
            q_all[g, core, j] = flat.astype(BF16)
        for d in range(1, CHIPS):
            q_copy(f, away(d), j).start()
            if DIRECT_Q[f]:
                q_cross(f, away(d)).start()
        q_forward(f, core, j).start()

    def forward_queries(f):
        for d in range(1, CHIPS):
            src = away(d)
            q_copy(f, src, src).wait_recv()
            if not DIRECT_Q[f]:
                q_forward(f, core, src).start()

    def await_queries(f):
        for slot in range(CHIPS):
            q_forward(f, other, slot).wait_recv()

    def prepare_bias():
        lane = lax.broadcasted_iota(jnp.int32, (SUB, HD), 1)
        sub = lax.broadcasted_iota(jnp.int32, (SUB, HD), 0)
        lane_sub = lax.rem(lane, SUB)
        lane_gran = lax.div(lane, SUB)
        position = lane_gran * ROWS + j * SUB + lane_sub
        key_row = j * SUB + lane_sub
        for jt in range(CHIPS):
            seen_by_row = jnp.zeros((SUB, HD), jnp.int32)
            for b in range(SUB):
                seen_by_row = jnp.where(sub == b, visible_ref[jt * SUB + b], seen_by_row)
            query_row = jt * SUB + sub
            for g in range(GRANULES):
                limit = g * ROWS + query_row + 1 if g < PROMPT_N else seen_by_row
                on_prompt = jnp.where((lane_gran < PROMPT_N) & (position < limit), 0.0, HIDDEN)
                if g < PROMPT_N:
                    on_steps = jnp.full((SUB, HD), HIDDEN, F32)
                else:
                    on_steps = jnp.where(
                        (lane_gran <= g - PROMPT_N) & (key_row == query_row), 0.0, HIDDEN
                    )
                bias[g, jt] = jnp.where(core == 0, on_prompt, on_steps)

    spread(0)
    spread_squares()
    a0_send[later_rows] = project(later_rows, other * WIDE).astype(BF16)
    for f in range(1, len(FRONT)):
        first(f).start()
    pairs = jnp.dot(xs[...], wkv[...], preferred_element_type=F32)
    pairs = pairs.reshape(GRANULES, CHIPS, SUB, 2 * HD)
    for i in range(PROMPT_N):
        of_prompt = pairs[i]
        of_steps = pairs[PROMPT_N + i] if i < STEPS else jnp.zeros((CHIPS, SUB, 2 * HD), F32)
        kv0_send[:, i] = jnp.where(core == 0, of_steps, of_prompt).astype(BF16)
        kvp[:, i] = jnp.where(core == 0, of_prompt, of_steps)
    kv_first.start()
    po[later_rows] = project(later_rows, core * WIDE)
    spread(1)
    square_sums()
    query_sums(0)
    spread_pairs()
    prepare_bias()
    key_load.wait()
    lax.fori_loop(0, TILES // 2, prepare_keys, 0)
    query_sums(1)
    spread(2)
    lax.fori_loop(TILES // 2, TILES, prepare_keys, 0)
    value_load.wait()
    lax.fori_loop(0, TILES, prepare_values, 0)
    forward_queries(0)
    pair_sums()
    await_queries(0)

    def lane_max(scores):
        high = scores[:, 0:HD]
        for u in range(1, scores.shape[1] // HD):
            high = jnp.maximum(high, scores[:, u * HD : (u + 1) * HD])
        return high

    def sweep(n_scores, top):
        if n_scores is not None:
            queries = q_all[n_scores].reshape(BLOCK, HD)
            mask = bias[n_scores].reshape(1, CHIPS, 1, SUB, HD)
        high = None
        mixed = None
        for t in range(TILES + 1):
            cols = slice(t * TILE, (t + 1) * TILE)
            if top is not None:
                old = s_buf[t] if t < TILES else sx_buf[...]
                weights = jnp.exp2(old - top).astype(BF16)
            if n_scores is not None:
                if t < TILES:
                    scores = jnp.dot(queries, k_t[:, cols], preferred_element_type=F32)
                    s_buf[t] = scores
                else:
                    scores = jnp.dot(queries, kx_t[...], preferred_element_type=F32)
                    scores = scores.reshape(2, CHIPS, HEADS, SUB, HD) + mask
                    scores = scores.reshape(BLOCK, HD)
                    sx_buf[...] = scores
                peak = lane_max(scores)
                high = peak if high is None else jnp.maximum(high, peak)
            if top is not None:
                values = v_x[cols] if t < TILES else vx_x[...]
                part = jnp.dot(weights, values, preferred_element_type=F32)
                mixed = part if mixed is None else mixed + part
        if n_scores is not None:
            mx[...] = high
        return mixed

    def split3(row):
        one = row.astype(BF16).astype(F32)
        two = (row - one).astype(BF16).astype(F32)
        return one, two, row - one - two

    def packed(mixture, top_row, total_row):
        sub = lax.broadcasted_iota(jnp.int32, (PACK - FLAT, HD), 0)
        stats = jnp.zeros((PACK - FLAT, HD), F32)
        for i, piece in enumerate(split3(top_row) + split3(total_row)):
            stats = jnp.where(sub == i, piece, stats)
        return jnp.concatenate([mixture, stats], axis=0).astype(BF16)

    def unpacked(packet):
        wide = packet.astype(F32)
        stats = wide[FLAT:]
        return (
            wide[0:FLAT],
            stats[0:1] + stats[1:2] + stats[2:3],
            stats[3:4] + stats[4:5] + stats[5:6],
        )

    def block_of(n, column, jt):
        rows = slice(jt * FLAT, (jt + 1) * FLAT)
        top_row = as_row(eye_flat, top_all[n, column, rows])
        total_row = as_row(eye_flat, mix_all[n, column, rows, HD:])
        return mix_all[n, column, rows, 0:HD], top_row, total_row

    def keep(n, mixed, top):
        mix_all[n] = mixed.reshape(2, HALF, 2 * HD)
        top_all[n] = jnp.broadcast_to(top, (BLOCK, HD)).reshape(2, HALF, HD)
        for jt in range(CHIPS):
            b0_send[n, jt] = packed(*block_of(n, other, jt))

    def b0_copy(b):
        grans = span(BACK[b])
        return remote(b0_send.at[grans], b0_recv.at[grans], b0_ss.at[b], b0_rs.at[b], sib)

    def b1_copy(b, jt, slot):
        grans = span(BACK[b])
        return remote(
            b1_send.at[jt, grans], b1_recv.at[slot, grans], b1_ss.at[b, jt], b1_rs.at[b, slot], chip(jt)
        )

    def merge_pair(b):
        b0_copy(b).wait_recv()
        g0, count = BACK[b]
        for g in range(g0, g0 + count):
            for jt in range(CHIPS):
                mix1, top1, tot1 = unpacked(b0_recv[g, jt])
                mix0, top0, tot0 = block_of(g, core, jt)
                top = jnp.maximum(top0, top1)
                w0 = jnp.exp2(top0 - top)
                w1 = jnp.exp2(top1 - top)
                mixture = mix0 * as_column(eye_flat, w0) + mix1 * as_column(eye_flat, w1)
                b1_send[jt, g] = packed(mixture, top, w0 * tot0 + w1 * tot1)
        for d in range(1, CHIPS):
            b1_copy(b, away(d), j).start()

    def att_at(b, column, slot):
        return att.at[column, span(BACK[b]), slot]

    def att_copy(b, jt, slot):
        return remote(
            att_at(b, core, slot), att_at(b, core, slot), ag_ss.at[b, jt], ag_rs.at[b, slot], chip(jt)
        )

    def att_cross(b, jt):
        return remote(
            att_at(b, core, j), att_at(b, core, j), af_ss.at[b, jt], af_rs.at[b, j], cross(jt)
        )

    def att_forward(b, column, slot):
        return remote(
            att_at(b, column, slot),
            att_at(b, column, slot),
            af_ss.at[b, slot],
            af_rs.at[b, slot],
            sib,
        )

    def merge_all(b):
        g0, count = BACK[b]
        for d in range(1, CHIPS):
            b1_copy(b, away(d), away(d)).wait_recv()
        for g in range(g0, g0 + count):
            pieces = [unpacked(b1_send[j, g])]
            for d in range(1, CHIPS):
                pieces.append(unpacked(b1_recv[away(d), g]))
            top = pieces[0][1]
            for piece in pieces[1:]:
                top = jnp.maximum(top, piece[1])
            shares = [jnp.exp2(piece[1] - top) for piece in pieces]
            total = shares[0] * pieces[0][2]
            for share, piece in zip(shares[1:], pieces[1:]):
                total = total + share * piece[2]
            result = jnp.zeros((FLAT, HD), F32)
            for share, piece in zip(shares, pieces):
                result = result + piece[0] * as_column(eye_flat, share)
            result = result * as_column(eye_flat, 1.0 / total)
            att[core, g, j] = jnp.concatenate(
                [result[h * SUB : (h + 1) * SUB] for h in range(HEADS)], axis=1
            ).astype(BF16)
        for d in range(1, CHIPS):
            att_copy(b, away(d), j).start()
            if DIRECT_A[b]:
                att_cross(b, away(d)).start()
        att_forward(b, core, j).start()

    def forward_attended(b):
        for d in range(1, CHIPS):
            src = away(d)
            att_copy(b, src, src).wait_recv()
            if not DIRECT_A[b]:
                att_forward(b, core, src).start()

    def await_attended(b):
        for slot in range(CHIPS):
            att_forward(b, other, slot).wait_recv()

    def out_part(g0, count, column):
        rows = att[column, g0 : g0 + count].astype(F32).reshape(count * ROWS, WIDE).astype(BF16)
        low = pl.multiple_of(column * WIDE, WIDE)
        return jnp.dot(rows, wo[pl.ds(low, WIDE)], preferred_element_type=F32)

    def cp_copy(kt, slot):
        return remote(cp_send.at[kt], cp_recv.at[slot], c_ss.at[0, kt], c_rs.at[0, slot], (c, kt))

    def cs_copy(low, high, kt, slot):
        i = 1 if low == 0 else 2
        return remote(
            cs_send.at[kt, low:high],
            cs_recv.at[slot, low:high],
            c_ss.at[i, kt],
            c_rs.at[i, slot],
            (c, kt),
        )

    def next_kv(d):
        return lax.rem(k + d, KV)

    def finish_prompt():
        result = out_part(0, PROMPT_N, core) + out_part(0, PROMPT_N, other)
        cp_send[...] = result.reshape(KV, PROMPT // KV, FEAT).astype(BF16)
        for d in range(1, KV):
            cp_copy(next_kv(d), k).start()

    def finish_steps(low, high):
        count = high - low
        result = out_part(PROMPT_N + low, count, core) + out_part(PROMPT_N + low, count, other)
        for s in range(count):
            piece = result[s * ROWS : (s + 1) * ROWS]
            cs_send[:, low + s] = piece.reshape(KV, SUB, FEAT).astype(BF16)
        for d in range(1, KV):
            cs_copy(low, high, next_kv(d), k).start()

    def write_prompt():
        final = cp_send[k].astype(F32)
        for d in range(1, KV):
            src = next_kv(d)
            cp_copy(src, src).wait_recv()
            final = final + cp_recv[src].astype(F32)
        prompt_out[...] = final.astype(BF16)

    def write_steps(low, high):
        final = cs_send[k, low:high].astype(F32)
        for d in range(1, KV):
            src = next_kv(d)
            cs_copy(low, high, src, src).wait_recv()
            final = final + cs_recv[src, low:high].astype(F32)
        step_out[low:high] = final.astype(BF16)

    def step_top():
        return jnp.max(mx[...], axis=1, keepdims=True)

    sweep(0, None)
    forward_queries(1)
    query_sums(2)

    def step(n, carry):
        @pl.when(n == 1)
        def _():
            await_queries(1)

        @pl.when(n == 2)
        def _():
            b0_copy(0).start()
            forward_queries(2)

        @pl.when(n == 3)
        def _():
            await_queries(2)
            merge_pair(0)

        @pl.when(n == 4)
        def _():
            b0_copy(1).start()
            merge_all(0)

        @pl.when(n == 5)
        def _():
            b0_copy(2).start()
            merge_pair(1)
            forward_attended(0)

        top = step_top()
        keep(n, sweep(n + 1, top), top)
        return carry

    last = GRANULES - 1
    lax.fori_loop(0, last, step, 0)
    b0_copy(3).start()
    merge_pair(2)
    merge_all(1)
    top = step_top()
    keep(last, sweep(None, top), top)
    b0_copy(4).start()
    merge_pair(3)
    merge_pair(4)
    merge_all(2)
    forward_attended(1)
    await_attended(0)
    await_attended(1)
    merge_all(3)
    merge_all(4)
    wo_load.wait()
    finish_prompt()
    forward_attended(2)
    forward_attended(3)
    await_attended(2)
    await_attended(3)
    finish_steps(0, STEPS - 1)
    forward_attended(4)
    await_attended(4)
    finish_steps(STEPS - 1, STEPS)
    write_prompt()
    write_steps(0, STEPS - 1)
    write_steps(STEPS - 1, STEPS)

    kv_first.wait_send()
    sq_first.wait_send()
    for f in range(len(FRONT)):
        first(f).wait_send()
        q_forward(f, core, j).wait_send()
    for b in range(len(BACK)):
        b0_copy(b).wait_send()
        att_forward(b, core, j).wait_send()
    for d in range(1, CHIPS):
        jt = away(d)
        sq1_copy(jt, j).wait_send()
        kv1_copy(jt, j).wait_send()
        cp_copy(next_kv(d), k).wait_send()
        cs_copy(0, STEPS - 1, next_kv(d), k).wait_send()
        cs_copy(STEPS - 1, STEPS, next_kv(d), k).wait_send()
        for f in range(len(FRONT)):
            a1_copy(f, jt, j).wait_send()
            q_copy(f, jt, j).wait_send()
            if DIRECT_Q[f]:
                q_cross(f, jt).wait_send()
            else:
                q_forward(f, core, jt).wait_send()
        for b in range(len(BACK)):
            b1_copy(b, jt, j).wait_send()
            att_copy(b, jt, j).wait_send()
            if DIRECT_A[b]:
                att_cross(b, jt).wait_send()
            else:
                att_forward(b, core, jt).wait_send()


def place_outputs(prompt_ref, step_ref, prompt_out, step_out):
    prompt_out[...] = prompt_ref[...]
    step_out[...] = step_ref[...]


def on_device(
    prompt_in,
    step_in,
    norm_gain,
    query_weight,
    key_weight,
    value_weight,
    out_weight,
    key_cache,
    value_cache,
    cache_lengths,
    visible,
):
    dma = pltpu.SemaphoreType.DMA
    hbm = pl.BlockSpec(memory_space=pl.ANY)
    smem = pl.BlockSpec(memory_space=pltpu.SMEM)
    vmem = pl.BlockSpec(memory_space=pltpu.VMEM)
    fronts, backs = len(FRONT), len(BACK)
    scratch = [
        pltpu.VMEM((ALL, FEAT), BF16),
        pltpu.VMEM((FEAT,), BF16),
        pltpu.VMEM((ALL, FEAT), BF16),
        pltpu.VMEM((FEAT, 2 * WIDE), BF16),
        pltpu.VMEM((FEAT, 2 * HD), BF16),
        pltpu.VMEM((2 * WIDE, FEAT), BF16),
        pltpu.VMEM((SLOTS, HD), BF16),
        pltpu.VMEM((HD, SLOTS), BF16),
        pltpu.VMEM((SLOTS, 2 * HD), BF16),
        pltpu.VMEM((HD, HD), BF16),
        pltpu.VMEM((HD, 2 * HD), BF16),
        pltpu.VMEM((GRANULES, CHIPS, SUB, HD), F32),
        pltpu.VMEM((OWN, HD), F32),
        pltpu.VMEM((ALL, WIDE), F32),
        pltpu.VMEM((CHIPS, PROMPT_N, SUB, 2 * HD), F32),
        pltpu.VMEM((ALL, WIDE), BF16),
        pltpu.VMEM((ALL, WIDE), BF16),
        pltpu.VMEM((CHIPS, PROMPT_N, SUB, 2 * HD), BF16),
        pltpu.VMEM((CHIPS, PROMPT_N, SUB, 2 * HD), BF16),
        pltpu.VMEM((CHIPS, 1, HD), F32),
        pltpu.VMEM((CHIPS, 1, HD), F32),
        pltpu.VMEM((CHIPS, GRANULES, SUB, WIDE), BF16),
        pltpu.VMEM((CHIPS, GRANULES, SUB, WIDE), BF16),
        pltpu.VMEM((CHIPS, PROMPT_N, SUB, 2 * HD), BF16),
        pltpu.VMEM((CHIPS, PROMPT_N, SUB, 2 * HD), BF16),
        pltpu.VMEM((CHIPS, 1, HD), F32),
        pltpu.VMEM((CHIPS, 1, HD), F32),
        pltpu.VMEM((GRANULES, 2, CHIPS, FLAT, HD), BF16),
        pltpu.VMEM((TILES, BLOCK, TILE), F32),
        pltpu.VMEM((BLOCK, HD), F32),
        pltpu.VMEM((BLOCK, HD), F32),
        pltpu.VMEM((GRANULES, 2, HALF, 2 * HD), F32),
        pltpu.VMEM((GRANULES, 2, HALF, HD), F32),
        pltpu.VMEM((GRANULES, CHIPS, PACK, HD), BF16),
        pltpu.VMEM((GRANULES, CHIPS, PACK, HD), BF16),
        pltpu.VMEM((CHIPS, GRANULES, PACK, HD), BF16),
        pltpu.VMEM((CHIPS, GRANULES, PACK, HD), BF16),
        pltpu.VMEM((2, GRANULES, CHIPS, SUB, WIDE), BF16),
        pltpu.VMEM((KV, PROMPT // KV, FEAT), BF16),
        pltpu.VMEM((KV, PROMPT // KV, FEAT), BF16),
        pltpu.VMEM((KV, STEPS, SUB, FEAT), BF16),
        pltpu.VMEM((KV, STEPS, SUB, FEAT), BF16),
        dma((9,)),
        dma((fronts + 2,)),
        dma((fronts + 2,)),
        dma((backs,)),
        dma((backs,)),
        dma((fronts, CHIPS)),
        dma((fronts, CHIPS)),
        dma((CHIPS,)),
        dma((CHIPS,)),
        dma((CHIPS,)),
        dma((CHIPS,)),
        dma((fronts, CHIPS)),
        dma((fronts, CHIPS)),
        dma((fronts, CHIPS)),
        dma((fronts, CHIPS)),
        dma((backs, CHIPS)),
        dma((backs, CHIPS)),
        dma((backs, CHIPS)),
        dma((backs, CHIPS)),
        dma((backs, CHIPS)),
        dma((backs, CHIPS)),
        dma((3, KV)),
        dma((3, KV)),
    ]
    shapes = (
        jax.ShapeDtypeStruct((PROMPT // KV, FEAT), BF16),
        jax.ShapeDtypeStruct((STEPS, SUB, FEAT), BF16),
    )
    results = pl.pallas_call(
        kernel,
        out_shape=shapes,
        in_specs=[hbm] * 9 + [smem] * 2,
        out_specs=(vmem, vmem),
        scratch_shapes=scratch,
        compiler_params=pltpu.CompilerParams(
            collective_id=0, has_side_effects=True, vmem_limit_bytes=58 * 2**20
        ),
    )(
        prompt_in,
        step_in.reshape(STEPS * ROWS, FEAT),
        norm_gain,
        query_weight,
        key_weight,
        value_weight,
        out_weight,
        key_cache.reshape(SLOTS, HD),
        value_cache.reshape(SLOTS, HD),
        cache_lengths,
        visible,
    )
    return pl.pallas_call(
        place_outputs, out_shape=shapes, in_specs=[vmem] * 2, out_specs=(vmem, vmem)
    )(*results)


def solution(mesh):
    placed = (
        P(None, "ctx"),
        P(None, None, "ctx"),
        P("ctx"),
        P("ctx", "kv"),
        P("ctx", "kv"),
        P("ctx", "kv"),
        P("kv", "ctx"),
        P("kv", "ctx", None),
        P("kv", "ctx", None),
        P("ctx"),
        P(),
    )
    return jax.shard_map(
        on_device,
        mesh=mesh,
        in_specs=placed,
        out_specs=(P("kv", "ctx"), P(None, "kv", "ctx")),
        check_vma=False,
    )
```
